256 devices in a mesh: dp: 64 (over x, z, core), tensor: 4 (over y).
Axes of the slice: x: 4, y: 4, z: 8, core: 2. Of those that a mesh axis runs over, the one named last changes fastest.
Arguments:
- cotangent: bfloat16 [16384, 4096], P(('dp', 'tensor')), may hold values from -6 to 6
- gate_pre: bfloat16 [16384, 1024], P('dp', 'tensor'), may hold values from -6 to 6
- up_pre: bfloat16 [16384, 1024], P('dp', 'tensor'), may hold values from -6 to 6
- down_weight: bfloat16 [1024, 4096], P('tensor'), may hold values from -0.1875 to 0.1875
- gate_weight: bfloat16 [4096, 1024], P(None, 'tensor'), may hold values from -0.09375 to 0.09375
- up_weight: bfloat16 [4096, 1024], P(None, 'tensor'), may hold values from -0.09375 to 0.09375
- error_in: bfloat16 [64, 1024, 4096], P('dp', 'tensor'), may hold values from -6 to 6
- factor_in: float32 [4, 64, 4096], P('tensor'), may hold values from -6 to 6
Outputs:
- input_grad: bfloat16 [16384, 4096], P(('dp', 'tensor'))
- left_out: float32 [1024, 64], P('tensor')
- right_mean: float32 [4, 64, 4096], P('tensor')
- error_out: bfloat16 [64, 1024, 4096], P('dp', 'tensor')
The draws below stay inside these ranges and needn't reach their ends.
All inputs are finite; a program needn't handle non-finite values.
Results may differ from the reference program's by a relative error of at most 0.013.
Values may be sent and summed in bfloat16 or wider, within the bound.
A program may use at most 64 MiB of HBM per device.

```python
import jax
import jax.numpy as jnp
from jax import lax

D = 4096
F_DEV = 256
RANK = 64
TOK_DEV = 256
F_ALL = 1024
TILES = 4
REPLICA_COUNT = 64
TOKENS = 16384
N_TENSOR = 4


def block_levels(key, dims, shards, least, largest):
    gain = 1.0
    for dim, blocks in shards:
        draws = jax.random.uniform(jax.random.fold_in(jax.random.fold_in(key, 6), dim), (blocks,), jnp.float32, least / len(shards), largest / len(shards))
        gain = gain * jnp.repeat(jnp.exp(draws), dims[dim] // blocks).reshape((-1,) + (1,) * (len(dims) - 1 - dim))
    return gain


def noise(own_key, shape, scale, bound, cuts=(), kind=jnp.bfloat16):
    entries = scale * jax.random.normal(own_key, shape, jnp.float32)
    if cuts:
        entries = entries * block_levels(own_key, shape, cuts, -0.22, 0.18)
    return jnp.clip(entries, -bound, bound).astype(kind)


def setup_inputs(seed: int = 0) -> dict:
    seeds = jax.random.split(jax.random.key(seed), 9)
    cotangent = noise(seeds[0], (TOKENS, D), 1.0, 6.0, ((0, 256),))
    gate_pre = noise(seeds[1], (TOKENS, F_ALL), 1.0, 6.0, ((0, 64), (1, 4)))
    up_pre = noise(seeds[2], (TOKENS, F_ALL), 1.0, 6.0, ((0, 64), (1, 4)))
    down_weight = noise(seeds[3], (F_ALL, D), F_ALL ** -0.5, 0.1875, ((0, 4),))
    gate_weight = noise(seeds[4], (D, F_ALL), D ** -0.5, 0.09375, ((1, 4),))
    up_weight = noise(seeds[5], (D, F_ALL), D ** -0.5, 0.09375, ((1, 4),))
    error_in = noise(seeds[6], (REPLICA_COUNT, F_ALL, D), 1.0, 6.0, ((0, 64), (1, 4)))
    factor_in = noise(seeds[7], (TILES, RANK, D), 1.0, 6.0, ((0, 4),), jnp.float32)
    return {"cotangent": cotangent, "gate_pre": gate_pre, "up_pre": up_pre, "down_weight": down_weight, "gate_weight": gate_weight, "up_weight": up_weight, "error_in": error_in, "factor_in": factor_in}


epsilon = 1e-06

def swiglu_back(grad_hidden, gate_pre, up_pre):
    gate_values = gate_pre.astype(jnp.float32)
    up_values = up_pre.astype(jnp.float32)
    sigmoid_gate = jax.nn.sigmoid(gate_values)
    silu_gate = gate_values * sigmoid_gate
    hidden = (silu_gate * up_values).astype(jnp.bfloat16)
    d_gate = (grad_hidden * up_values * sigmoid_gate * (1.0 + gate_values * (1.0 - sigmoid_gate))).astype(jnp.bfloat16)
    d_up = (grad_hidden * silu_gate).astype(jnp.bfloat16)
    return (hidden, d_gate, d_up)

def orthonormal(matrix):
    count_rows = matrix.shape[0]

    def step(column, current_tile):
        vector = lax.dynamic_index_in_dim(current_tile, column, 0, keepdims=False)
        vector = vector / jnp.sqrt(jnp.sum(vector * vector) + epsilon)
        correlation = jnp.dot(current_tile, vector, precision=lax.Precision.HIGHEST)
        later_rows = jnp.arange(count_rows) > column
        current_tile = current_tile - jnp.where(later_rows, correlation, jnp.zeros_like(correlation))[:, None] * vector[None, :]
        return lax.dynamic_update_index_in_dim(current_tile, vector, column, 0)
    return lax.fori_loop(0, count_rows, step, matrix)

def reference(cotangent, gate_pre, up_pre, down_weight, gate_weight, up_weight, error_in, factor_in):

    def replica(replica_index):
        row_start = (replica_index * TOK_DEV).astype(jnp.int32)
        block_of_rows = lax.dynamic_slice_in_dim(cotangent, row_start, TOK_DEV, 0)
        gate_block = lax.dynamic_slice_in_dim(gate_pre, row_start, TOK_DEV, 0)
        up_block = lax.dynamic_slice_in_dim(up_pre, row_start, TOK_DEV, 0)
        grad_hidden = lax.dot_general(block_of_rows, down_weight, (((1,), (1,)), ((), ())), preferred_element_type=jnp.float32)
        hidden, d_gate, d_up = swiglu_back(grad_hidden, gate_block, up_block)
        summed_parts = jnp.zeros((TOK_DEV, D), jnp.float32)
        for tile_index in range(N_TENSOR):
            low = tile_index * F_DEV
            high = low + F_DEV
            partial_value = lax.dot_general(d_gate[:, low:high], gate_weight[:, low:high], (((1,), (1,)), ((), ())), preferred_element_type=jnp.float32)
            partial_value = partial_value + lax.dot_general(d_up[:, low:high], up_weight[:, low:high], (((1,), (1,)), ((), ())), preferred_element_type=jnp.float32)
            rounded = lax.optimization_barrier(partial_value.astype(jnp.bfloat16))
            summed_parts = summed_parts + rounded.astype(jnp.float32)
        weight_grad = lax.dot_general(hidden, block_of_rows, (((0,), (0,)), ((), ())), preferred_element_type=jnp.float32)
        weight_grad = weight_grad + lax.dynamic_index_in_dim(error_in, replica_index, 0, keepdims=False).astype(jnp.float32)
        return (summed_parts.astype(jnp.bfloat16), weight_grad)
    input_blocks, grads = lax.map(replica, jnp.arange(REPLICA_COUNT, dtype=jnp.int32))
    input_grad = input_blocks.reshape(TOKENS, D)
    tile_blocks = grads.reshape(REPLICA_COUNT, TILES, F_DEV, D)
    left_sum = jnp.einsum('itfd,trd->tfr', tile_blocks, factor_in, precision=lax.Precision.HIGHEST) / REPLICA_COUNT
    orthonormal_rows = jax.vmap(orthonormal)(jnp.swapaxes(left_sum, 1, 2))
    right_mean = jnp.einsum('lkeh,kae->kah', tile_blocks, orthonormal_rows, precision=lax.Precision.HIGHEST) / REPLICA_COUNT
    approximation = jnp.einsum('lxn,lxz->lnz', orthonormal_rows, right_mean, precision=lax.Precision.HIGHEST)
    error_out = (tile_blocks - approximation[None]).reshape(REPLICA_COUNT, F_ALL, D).astype(jnp.bfloat16)
    left_out = jnp.swapaxes(orthonormal_rows, 1, 2).reshape(F_ALL, RANK)
    return (input_grad, left_out, right_mean, error_out)
```

```python
import functools

import jax
import jax.numpy as jnp
from jax import lax
from jax.experimental import pallas as pl
from jax.experimental.pallas import tpu as pltpu
from jax.sharding import PartitionSpec as P

epsilon = 1e-06
NX, NZ, NC = 4, 8, 2
NY = 4
MESH = pl.DeviceIdType.MESH
f32, bf16 = jnp.float32, jnp.bfloat16
NN = (((1,), (0,)), ((), ()))
NT = (((1,), (1,)), ((), ()))


def dot(a, b, dims=NN):
    return lax.dot_general(a, b, dims, preferred_element_type=f32)


def split(a):
    high = a.astype(bf16)
    low = (a - high.astype(f32)).astype(bf16)
    return jnp.concatenate([high, low], axis=0)


def fold(a):
    half = a.shape[0] // 2
    return a[:half] + a[half:]


def kernel(
    c, gate, up, wd, wg, wu, e, f,
    ig, left_out, right_out, err,
    cbuf, wd_v, wg_v, wu_v, e_v, f_v, fs, gate_v, up_v, hid, hid_t, y_v, pe, dg, du,
    part, ig_in, ig_sum, ig_v,
    p1, p1_in, p2_in, t_v, ts, tt, zs, m_v,
    r1, r1_in, r2, r2_in, r3, r4_in, right_v, err_v,
    load, ag_s, ag_r, p1_s, p1_r, p2_s, p2_r, p3_s, p3_r,
    r1_s, r1_r, r2_s, r2_r, r3_s, r3_r, r4_s, r4_r, ig_s, ig_r, out_s,
):
    G = NX * NC
    rows, D = c.shape
    half = rows // 2
    TOK = NY * rows
    F = wd.shape[0]
    RANK = f.shape[0]
    prow = RANK // G
    HC = G // 4
    zw = D // HC // NZ
    width = 512 if D >= 4096 else 256

    dp, y = lax.axis_index("dp"), lax.axis_index("tensor")
    core = lax.rem(dp, NC)
    z = lax.rem(dp // NC, NZ)
    x = dp // (NC * NZ)
    g = x * NC + core
    y_right, y_left, y_opp = (lax.rem(y + k, NY) for k in (1, 3, 2))

    def in_group(d):
        other = lax.rem(g + d, G)
        return (((other // NC) * NZ + z) * NC + lax.rem(other, NC), y)

    def in_z(d):
        return ((x * NZ + lax.rem(z + d, NZ)) * NC + core, y)

    mine = cbuf.at[y]
    pairs = [(c, mine), (f, f_v), (e, e_v), (gate, gate_v), (up, up_v), (wd, wd_v), (wg, wg_v), (wu, wu_v)]
    loads = [pltpu.make_async_copy(a, b, load.at[k]) for k, (a, b) in enumerate(pairs)]
    for copy in loads:
        copy.start()

    barrier = pltpu.get_barrier_semaphore()
    partners = [(dp, y_right), (dp, y_left)]
    partners += [in_group(d) for d in range(1, G)] + [in_z(d) for d in range(1, NZ)]
    for other in partners:
        pl.semaphore_signal(barrier, inc=1, device_id=other, device_id_type=MESH)
    pl.semaphore_wait(barrier, len(partners))

    def send(src, dst, s, r, to):
        copy = pltpu.make_async_remote_copy(
            src_ref=src, dst_ref=dst, send_sem=s, recv_sem=r, device_id=to, device_id_type=MESH
        )
        copy.start()
        return copy

    sent = []
    right, left = (dp, y_right), (dp, y_left)
    A, B = pl.ds(0, half), pl.ds(half, half)

    def gather(k, src, dst, to):
        copy = send(src, dst, ag_s.at[k], ag_r.at[k], to)
        sent.append(copy)
        return copy

    from_left_a = gather(0, c.at[A], cbuf.at[y, A], right)
    from_right_b = gather(1, c.at[B], cbuf.at[y, B], left)
    from_left_b = gather(2, c.at[B], cbuf.at[y, B], right)
    from_right_a = gather(3, c.at[A], cbuf.at[y, A], left)

    loads[1].wait()
    fs[...] = split(f_v[...])
    loads[0].wait()

    def tokens_times_factor(slot):
        both = dot(cbuf[slot], fs[...], NT)
        y_v[slot] = both[:, :RANK] + both[:, RANK:]

    tokens_times_factor(y)
    loads[2].wait()
    pe[...] = fold(dot(fs[...], e_v[...], NT))
    loads[3].wait()
    loads[4].wait()
    a, u = gate_v[...].astype(f32), up_v[...].astype(f32)
    hidden = a * jax.nn.sigmoid(a) * u
    hidden = hidden.astype(bf16).astype(f32)
    hid[...] = hidden.astype(bf16)
    hid_t[...] = hidden.T.astype(bf16)

    from_left_a.wait_recv()
    from_opp_a = gather(4, cbuf.at[y_left, A], cbuf.at[y_left, A], right)
    from_right_b.wait_recv()
    from_opp_b = gather(5, cbuf.at[y_right, B], cbuf.at[y_right, B], left)
    from_left_b.wait_recv()
    tokens_times_factor(y_left)
    from_right_a.wait_recv()
    tokens_times_factor(y_right)
    from_opp_a.wait_recv()
    from_opp_b.wait_recv()
    tokens_times_factor(y_opp)

    y_all = y_v[...].reshape(TOK, RANK)
    y_high = y_all.astype(bf16).astype(f32)
    y_both = jnp.concatenate([y_high, y_all - y_high], axis=1).T.astype(bf16)
    p_all = fold(dot(y_both, hid[...])) + pe[...]
    p1[...] = p_all.reshape(G, prow, F)

    p1_copies = []
    for d in range(1, G):
        other = lax.rem(g + d, G)
        p1_copies.append(send(p1.at[other], p1_in.at[g], p1_s.at[d], p1_r.at[d], in_group(d)))
    p1_in[g] = p1[g]

    loads[5].wait()
    grad = dot(cbuf[...].reshape(TOK, D), wd_v[...], NT)
    a, u = gate_v[...].astype(f32), up_v[...].astype(f32)
    s = jax.nn.sigmoid(a)
    dg[...] = (grad * u * s * (1.0 + a * (1.0 - s))).astype(bf16)
    du[...] = (grad * (a * s)).astype(bf16)

    for copy in p1_copies:
        copy.wait_recv()
    total = p1_in[0]
    for k in range(1, G):
        total = total + p1_in[k]
    p2_in[z] = total
    p2_copies = [
        send(p2_in.at[z], p2_in.at[z], p2_s.at[d], p2_r.at[d], in_z(d)) for d in range(1, NZ)
    ]

    loads[6].wait()
    loads[7].wait()

    @pl.loop(0, D // width)
    def _(j):
        here = pl.ds(pl.multiple_of(j * width, width), width)
        value = dot(dg[...], wg_v[here, :], NT) + dot(du[...], wu_v[here, :], NT)
        part[:, :, here] = value.astype(bf16).reshape(NY, rows, width)

    def give(k, src, to):
        sent.append(send(src, ig_in.at[k], ig_s.at[k], ig_r.at[k], to))
        return sent[-1]

    ig0 = give(0, part.at[y_opp, A], right)
    ig3 = give(3, part.at[y_opp, B], left)
    ig1 = give(1, part.at[y_right, B], right)
    ig4 = give(4, part.at[y_left, A], left)

    for copy in p2_copies:
        copy.wait_recv()
    total = p2_in[0]
    for k in range(1, NZ):
        total = total + p2_in[k]
    t_v[g] = total
    p3_copies = [
        send(t_v.at[g], t_v.at[g], p3_s.at[d], p3_r.at[d], in_group(d)) for d in range(1, G)
    ]

    @pl.loop(0, D // width)
    def _(j):
        here = pl.ds(pl.multiple_of(j * width, width), width)
        block = cbuf[:, :, here].reshape(TOK, width)
        m_v[:, here] = dot(hid_t[...], block) + e_v[:, here].astype(f32)

    for copy in p3_copies:
        copy.wait_recv()
    for copy in p3_copies:
        copy.wait_send()

    row_ids = lax.broadcasted_iota(jnp.int32, (RANK, 1), 0)
    tt[...] = t_v[...].reshape(RANK, F) * (1.0 / (NX * NZ * NC))

    def column(k, carry):
        vector = tt[pl.ds(k, 1), :]
        tile = tt[...]
        squares = jnp.sum(vector * vector, axis=1, keepdims=True) + epsilon
        factors = jnp.sum(tile * vector, axis=1, keepdims=True) * (1.0 / squares)
        tt[...] = tile - jnp.where(row_ids > k, factors, 0.0) * vector
        tt[pl.ds(k, 1), :] = vector * lax.rsqrt(squares)
        return carry

    lax.fori_loop(0, RANK, column, 0)
    left_copy = pltpu.make_async_copy(tt, left_out, out_s.at[0])
    left_copy.start()

    ts[...] = split(tt[...])
    zs[...] = split(fold(dot(ts[...], hid[...], NT)))

    r1_copies = []
    for h in range(HC):

        @pl.loop(0, D // HC // width)
        def _(j, h=h):
            start = pl.multiple_of(j * width, width)
            here = pl.ds(pl.multiple_of(h * (D // HC) + start, width), width)
            block = cbuf[:, :, here].reshape(TOK, width)
            value = fold(dot(zs[...], block) + dot(ts[...], e_v[:, here]))
            r1[pl.ds(4 * h, 4), :, pl.ds(start, width)] = value.astype(bf16).reshape(4, 16, width)

    for d in range(1, G):
        other = lax.rem(g + d, G)
        r1_copies.append(send(r1.at[other], r1_in.at[g], r1_s.at[d], r1_r.at[d], in_group(d)))
    r1_in[g] = r1[g]

    ig0.wait_recv()
    ig_sum[0] = (ig_in[0].astype(f32) + part[y_right, A].astype(f32)).astype(bf16)
    ig2 = give(2, ig_sum.at[0], right)
    ig3.wait_recv()
    ig_sum[1] = (ig_in[3].astype(f32) + part[y_left, B].astype(f32)).astype(bf16)
    ig5 = give(5, ig_sum.at[1], left)

    tt_both = jnp.concatenate([ts[:RANK].astype(f32), ts[RANK:].astype(f32)], axis=0).T.astype(bf16)

    for copy in r1_copies:
        copy.wait_recv()
    total = r1_in[0].astype(f32)
    for k in range(1, G):
        total = total + r1_in[k].astype(f32)
    for k in range(NZ):
        r2[k] = total[:, k * zw : (k + 1) * zw].astype(bf16)
    r2_copies = []
    for d in range(1, NZ):
        other = lax.rem(z + d, NZ)
        r2_copies.append(send(r2.at[other], r2_in.at[z], r2_s.at[d], r2_r.at[d], in_z(d)))
    r2_in[z] = r2[z]
    for copy in r2_copies:
        copy.wait_recv()
    total = r2_in[0].astype(f32)
    for k in range(1, NZ):
        total = total + r2_in[k].astype(f32)
    r3[z] = (total * (1.0 / (NX * NZ * NC))).astype(bf16)
    r3_copies = [
        send(r3.at[z], r3.at[z], r3_s.at[d], r3_r.at[d], in_z(d)) for d in range(1, NZ)
    ]
    for copy in r3_copies:
        copy.wait_recv()
    r4_copies = [
        send(r3, r4_in.at[g], r4_s.at[d], r4_r.at[d], in_group(d)) for d in range(1, G)
    ]
    r4_in[g] = r3[...]

    ig1.wait_recv()
    ig2.wait_recv()
    ig4.wait_recv()
    ig5.wait_recv()
    own_a = part[y, A].astype(f32) + ig_in[2].astype(f32) + ig_in[4].astype(f32)
    own_b = part[y, B].astype(f32) + ig_in[1].astype(f32) + ig_in[5].astype(f32)
    ig_v[A] = own_a.astype(bf16)
    ig_v[B] = own_b.astype(bf16)
    ig_copy = pltpu.make_async_copy(ig_v, ig, out_s.at[1])
    ig_copy.start()

    for copy in r4_copies:
        copy.wait_recv()

    for h in range(HC):

        @pl.loop(0, NZ)
        def _(k, h=h):
            here = pl.ds(pl.multiple_of(h * (D // HC) + k * zw, zw), zw)
            block = jnp.concatenate([r4_in[q + 4 * h, k] for q in range(4)], axis=0)
            right_v[:, here] = block.astype(f32)
            err_v[:, here] = (
                m_v[:, here] - dot(tt_both, jnp.concatenate([block, block], axis=0))
            ).astype(bf16)

    right_copy = pltpu.make_async_copy(right_v, right_out, out_s.at[2])
    right_copy.start()
    err_copy = pltpu.make_async_copy(err_v, err, out_s.at[3])
    err_copy.start()
    for copy in sent + p1_copies + p2_copies + r1_copies + r2_copies + r3_copies + r4_copies:
        copy.wait_send()
    for copy in (left_copy, ig_copy, right_copy, err_copy):
        copy.wait()


def shards(cotangent, gate_pre, up_pre, down_weight, gate_weight, up_weight, error_in, factor_in):
    G = NX * NC
    rows, D = cotangent.shape
    half = rows // 2
    TOK = NY * rows
    F = down_weight.shape[0]
    RANK = factor_in.shape[1]
    HC = G // 4
    zw = D // HC // NZ
    hw = D // HC
    VM = pltpu.VMEM
    DMA = pltpu.SemaphoreType.DMA
    scratch = [
        VM((NY, rows, D), bf16), VM((F, D), bf16), VM((D, F), bf16), VM((D, F), bf16),
        VM((F, D), bf16), VM((RANK, D), f32), VM((2 * RANK, D), bf16),
        VM((TOK, F), bf16), VM((TOK, F), bf16), VM((TOK, F), bf16), VM((F, TOK), bf16),
        VM((NY, rows, RANK), f32), VM((RANK, F), f32), VM((TOK, F), bf16), VM((TOK, F), bf16),
        VM((NY, rows, D), bf16), VM((6, half, D), bf16), VM((2, half, D), bf16), VM((rows, D), bf16),
        VM((G, RANK // G, F), f32), VM((G, RANK // G, F), f32), VM((NZ, RANK // G, F), f32),
        VM((G, RANK // G, F), f32), VM((2 * RANK, F), bf16), VM((RANK, F), f32),
        VM((2 * RANK, TOK), bf16), VM((F, D), f32),
        VM((G, 16, hw), bf16), VM((G, 16, hw), bf16), VM((NZ, 16, zw), bf16), VM((NZ, 16, zw), bf16),
        VM((NZ, 16, zw), bf16), VM((G, NZ, 16, zw), bf16), VM((RANK, D), f32), VM((F, D), bf16),
        DMA((8,)), DMA((6,)), DMA((6,)),
        DMA((G,)), DMA((G,)), DMA((NZ,)), DMA((NZ,)), DMA((G,)), DMA((G,)),
        DMA((G,)), DMA((G,)), DMA((NZ,)), DMA((NZ,)), DMA((NZ,)), DMA((NZ,)), DMA((G,)), DMA((G,)),
        DMA((6,)), DMA((6,)), DMA((4,)),
    ]
    shape = jax.ShapeDtypeStruct
    input_grad, left_t, right, error_out = pl.pallas_call(
        kernel,
        out_shape=(shape((rows, D), bf16), shape((RANK, F), f32), shape((RANK, D), f32), shape((F, D), bf16)),
        in_specs=[pl.BlockSpec(memory_space=pl.ANY)] * 8,
        out_specs=(pl.BlockSpec(memory_space=pl.ANY),) * 4,
        scratch_shapes=scratch,
        compiler_params=pltpu.CompilerParams(
            collective_id=0, has_side_effects=True, vmem_limit_bytes=48 * 1024 * 1024
        ),
        cost_estimate=pl.CostEstimate(flops=4 * 10**9, bytes_accessed=17 * 10**6, transcendentals=10**5),
    )(cotangent, gate_pre, up_pre, down_weight, gate_weight, up_weight, error_in[0], factor_in[0])
    return (input_grad, left_t.T, right[None], error_out[None])


def solution(mesh):
    in_specs = (
        P(("dp", "tensor"), None),
        P("dp", "tensor"),
        P("dp", "tensor"),
        P("tensor", None),
        P(None, "tensor"),
        P(None, "tensor"),
        P("dp", "tensor", None),
        P("tensor", None, None),
    )
    out_specs = (
        P(("dp", "tensor"), None),
        P("tensor", None),
        P("tensor", None, None),
        P("dp", "tensor", None),
    )
    return jax.shard_map(shards, mesh=mesh, in_specs=in_specs, out_specs=out_specs, check_vma=False)
```

```python
import functools

import jax
import jax.numpy as jnp
from jax import lax
from jax.experimental import pallas as pl
from jax.experimental.pallas import tpu as pltpu
from jax.sharding import PartitionSpec as P

epsilon = 1e-06
NX, NZ, NC = 4, 8, 2
NY = 4
VMEM_MIB = 57
MESH = pl.DeviceIdType.MESH
f32, bf16 = jnp.float32, jnp.bfloat16
NN = (((1,), (0,)), ((), ()))
NT = (((1,), (1,)), ((), ()))


def dot(a, b, dims=NN):
    return lax.dot_general(a, b, dims, preferred_element_type=f32)


def split(a):
    high = a.astype(bf16)
    low = (a - high.astype(f32)).astype(bf16)
    return jnp.concatenate([high, low], axis=0)


def fold(a):
    half = a.shape[0] // 2
    return a[:half] + a[half:]


def kernel(
    c, gate, up, wd, wg, wu, e, f,
    ig_v, tt, rfull, m_v,
    cbuf, wd_v, wg_v, wu_v, e_v, f_v, fs, gate_v, up_v, hid, hid_t, y_v, pe, dg, du,
    part, ig_in, ig_sum,
    p1, p1_in, p2_in, t_v, ts, mc, mc_in, mx, mx_in, r2, r2_in,
    load, ag_s, ag_r, p1_s, p1_r, p2_s, p2_r, p3_s, p3_r,
    mc_s, mc_r, mx_s, mx_r, r2_s, r2_r, r3_s, r3_r, r4_s, r4_r, r5_s, r5_r, ig_s, ig_r,
):
    G = NX * NC
    rows, D = c.shape
    half = rows // 2
    TOK = NY * rows
    F = wd.shape[0]
    RANK = f.shape[0]
    hw = D // NC
    xw = hw // NX
    zw = xw // (NZ // 4)
    width = min(1024, hw)
    mean = 1.0 / (NX * NZ * NC)

    dp, y = lax.axis_index("dp"), lax.axis_index("tensor")
    core = lax.rem(dp, NC)
    z = lax.rem(dp // NC, NZ)
    x = dp // (NC * NZ)
    g = x * NC + core
    y_right, y_left, y_opp = (lax.rem(y + k, NY) for k in (1, 3, 2))

    def in_group(d):
        other = lax.rem(g + d, G)
        return (((other // NC) * NZ + z) * NC + lax.rem(other, NC), y)

    def in_x(d):
        return ((lax.rem(x + d, NX) * NZ + z) * NC + core, y)

    def in_z(d):
        return ((x * NZ + lax.rem(z + d, NZ)) * NC + core, y)

    sibling = (dp + 1 - 2 * core, y)

    mine = cbuf.at[y]
    pairs = [(c, mine), (f, f_v), (e, e_v), (gate, gate_v), (up, up_v), (wd, wd_v), (wg, wg_v), (wu, wu_v)]
    loads = [pltpu.make_async_copy(a, b, load.at[k]) for k, (a, b) in enumerate(pairs)]
    for copy in loads:
        copy.start()

    barrier = pltpu.get_barrier_semaphore()
    partners = [(dp, y_right), (dp, y_left)]
    partners += [in_group(d) for d in range(1, G)] + [in_z(d) for d in range(1, NZ)]
    for other in partners:
        pl.semaphore_signal(barrier, inc=1, device_id=other, device_id_type=MESH)
    pl.semaphore_wait(barrier, len(partners))

    sent = []

    def send(src, dst, s, r, to):
        copy = pltpu.make_async_remote_copy(
            src_ref=src, dst_ref=dst, send_sem=s, recv_sem=r, device_id=to, device_id_type=MESH
        )
        copy.start()
        sent.append(copy)
        return copy

    right, left = (dp, y_right), (dp, y_left)
    A, B = pl.ds(0, half), pl.ds(half, half)

    def gather(k, src, dst, to):
        return send(src, dst, ag_s.at[k], ag_r.at[k], to)

    from_left_a = gather(0, c.at[A], cbuf.at[y, A], right)
    from_right_b = gather(1, c.at[B], cbuf.at[y, B], left)

    loads[1].wait()
    fs[...] = split(f_v[...])
    loads[0].wait()

    def tokens_times_factor(slot):
        both = dot(cbuf[slot], fs[...], NT)
        y_v[slot] = both[:, :RANK] + both[:, RANK:]

    tokens_times_factor(y)
    loads[2].wait()
    pe[...] = fold(dot(fs[...], e_v[...], NT))

    from_left_b = gather(2, c.at[B], cbuf.at[y, B], right)
    from_right_a = gather(3, c.at[A], cbuf.at[y, A], left)

    loads[3].wait()
    loads[4].wait()
    a, u = gate_v[...].astype(f32), up_v[...].astype(f32)
    hidden = a * jax.nn.sigmoid(a) * u
    hidden = hidden.astype(bf16).astype(f32)
    hid[...] = hidden.astype(bf16)
    hid_t[...] = hidden.T.astype(bf16)

    from_left_a.wait_recv()
    from_opp_a = gather(4, cbuf.at[y_left, A], cbuf.at[y_left, A], right)
    from_right_b.wait_recv()
    from_opp_b = gather(5, cbuf.at[y_right, B], cbuf.at[y_right, B], left)
    from_left_b.wait_recv()
    tokens_times_factor(y_left)
    from_right_a.wait_recv()
    tokens_times_factor(y_right)
    for k in (5, 6, 7):
        loads[k].wait()
    from_opp_a.wait_recv()
    from_opp_b.wait_recv()
    tokens_times_factor(y_opp)

    y_all = y_v[...].reshape(TOK, RANK)
    y_high = y_all.astype(bf16).astype(f32)
    y_both = jnp.concatenate([y_high, y_all - y_high], axis=1).T.astype(bf16)
    p_all = fold(dot(y_both, hid[...])) + pe[...]
    p1[...] = p_all.reshape(NZ, RANK // NZ, F)
    p1_copies = []
    for d in range(1, NZ):
        other = lax.rem(z + d, NZ)
        p1_copies.append(send(p1.at[other], p1_in.at[z], p1_s.at[d], p1_r.at[d], in_z(d)))
    p1_in[z] = p1[z]

    def weight_gradient(first, j):
        here = pl.ds(pl.multiple_of(first + j * width, width), width)
        block = cbuf[:, :, here].reshape(TOK, width)
        value = dot(hid_t[...], block) + e_v[:, here].astype(f32)
        m_v[:, here] = value
        return value

    for j in range(hw // width):
        mc[:, j * width : (j + 1) * width] = weight_gradient((1 - core) * hw, j).astype(bf16)
    mc_copy = send(mc, mc_in, mc_s.at[0], mc_r.at[0], sibling)
    for j in range(hw // width):
        weight_gradient(core * hw, j)

    grad = dot(cbuf[...].reshape(TOK, D), wd_v[...], NT)
    a, u = gate_v[...].astype(f32), up_v[...].astype(f32)
    s = jax.nn.sigmoid(a)
    dg[...] = (grad * u * s * (1.0 + a * (1.0 - s))).astype(bf16)
    du[...] = (grad * (a * s)).astype(bf16)
    for j in range(D // width):
        here = pl.ds(j * width, width)
        value = dot(dg[...], wg_v[here, :], NT) + dot(du[...], wu_v[here, :], NT)
        part[:, :, here] = value.astype(bf16).reshape(NY, rows, width)

    def give(k, src, to):
        return send(src, ig_in.at[k], ig_s.at[k], ig_r.at[k], to)

    ig0 = give(0, part.at[y_opp, A], right)
    ig3 = give(3, part.at[y_opp, B], left)

    def total_of(ref, count):
        total = ref[0].astype(f32)
        for k in range(1, count):
            total = total + ref[k].astype(f32)
        return total

    for copy in p1_copies:
        copy.wait_recv()
    p2_in[g] = total_of(p1_in, NZ)
    p2_copies = [
        send(p2_in.at[g], p2_in.at[g], p2_s.at[d], p2_r.at[d], in_group(d)) for d in range(1, G)
    ]
    ig1 = give(1, part.at[y_right, B], right)
    ig4 = give(4, part.at[y_left, A], left)

    mc_copy.wait_recv()
    for k in range(NX):
        here = pl.ds(pl.multiple_of(core * hw + k * xw, xw), xw)
        mx[k] = (m_v[:, here] + mc_in[:, k * xw : (k + 1) * xw].astype(f32)).astype(bf16)
    mx_copies = []
    for d in range(1, NX):
        other = lax.rem(x + d, NX)
        mx_copies.append(send(mx.at[other], mx_in.at[x], mx_s.at[d], mx_r.at[d], in_x(d)))
    mx_in[x] = mx[x]

    for copy in p2_copies:
        copy.wait_recv()
    for copy in p2_copies:
        copy.wait_send()
    t_v[z] = total_of(p2_in, G)
    p3_copies = [
        send(t_v.at[z], t_v.at[z], p3_s.at[d], p3_r.at[d], in_z(d)) for d in range(1, NZ)
    ]
    for copy in p3_copies:
        copy.wait_recv()

    row_ids = lax.broadcasted_iota(jnp.int32, (RANK, 1), 0)
    tt[...] = t_v[...].reshape(RANK, F) * mean

    def column(k, carry):
        vector = tt[pl.ds(k, 1), :]
        tile = tt[...]
        squares = jnp.sum(vector * vector, axis=1, keepdims=True) + epsilon
        factors = jnp.sum(tile * vector, axis=1, keepdims=True) * (1.0 / squares)
        tt[...] = tile - jnp.where(row_ids > k, factors, 0.0) * vector
        tt[pl.ds(k, 1), :] = vector * lax.rsqrt(squares)
        return carry

    lax.fori_loop(0, RANK, column, 0)
    ts[...] = split(tt[...])

    for copy in mx_copies:
        copy.wait_recv()
    m_sum = total_of(mx_in, NX)
    m_high = m_sum.astype(bf16)
    m_low = (m_sum - m_high.astype(f32)).astype(bf16)
    r_all = fold(dot(ts[...], m_high)) + dot(ts[:RANK], m_low)
    for k in range(NZ):
        q, h = k % 4, k // 4
        r2[k] = r_all[16 * q : 16 * q + 16, h * zw : (h + 1) * zw].astype(bf16)
    r2_copies = []
    for d in range(1, NZ):
        other = lax.rem(z + d, NZ)
        r2_copies.append(send(r2.at[other], r2_in.at[z], r2_s.at[d], r2_r.at[d], in_z(d)))
    r2_in[z] = r2[z]

    ig0.wait_recv()
    ig_sum[0] = (ig_in[0].astype(f32) + part[y_right, A].astype(f32)).astype(bf16)
    ig2 = give(2, ig_sum.at[0], right)
    ig3.wait_recv()
    ig_sum[1] = (ig_in[3].astype(f32) + part[y_left, B].astype(f32)).astype(bf16)
    ig5 = give(5, ig_sum.at[1], left)

    for copy in r2_copies:
        copy.wait_recv()
    rfull[core, x, z] = (total_of(r2_in, NZ) * mean).astype(bf16)
    own = rfull.at[core, x, z]
    r3_copies = [send(own, own, r3_s.at[d], r3_r.at[d], in_z(d)) for d in range(1, NZ)]
    for copy in r3_copies:
        copy.wait_recv()
    own = rfull.at[core, x]
    r4_copies = [send(own, own, r4_s.at[d], r4_r.at[d], in_x(d)) for d in range(1, NX)]
    r5_copies = [send(own, own, r5_s.at[0], r5_r.at[0], sibling)]

    ig1.wait_recv()
    ig4.wait_recv()
    ig2.wait_recv()
    own_a = part[y, A].astype(f32) + ig_in[2].astype(f32) + ig_in[4].astype(f32)
    ig_v[A] = own_a.astype(bf16)
    ig5.wait_recv()
    own_b = part[y, B].astype(f32) + ig_in[1].astype(f32) + ig_in[5].astype(f32)
    ig_v[B] = own_b.astype(bf16)

    for d in range(1, NX):
        r4_copies[d - 1].wait_recv()
        came = rfull.at[core, lax.rem(x + NX - d, NX)]
        r5_copies.append(send(came, came, r5_s.at[d], r5_r.at[d], sibling))
    for copy in r5_copies:
        copy.wait_recv()
    for copy in sent:
        if not any(copy is done for done in p2_copies):
            copy.wait_send()


def finish(ig_v, tt, rfull, m_v, ig, left_out, right_out, err, right_v, err_v, sems):
    RANK, F = tt.shape
    D = m_v.shape[1]
    hw = D // NC
    xw = hw // NX
    zw = xw // (NZ // 4)
    copies = [
        pltpu.make_async_copy(ig_v, ig, sems.at[0]),
        pltpu.make_async_copy(tt, left_out, sems.at[1]),
    ]
    for copy in copies:
        copy.start()
    high = tt[...].astype(bf16).astype(f32)
    both = jnp.concatenate([high, tt[...] - high], axis=0).T.astype(bf16)
    for k in range(NC * NX):
        first = k * xw
        blocks = []
        for h in range(NZ // 4):
            rows = [rfull[k // NX, k % NX, 4 * h + q] for q in range(4)]
            blocks.append(jnp.concatenate(rows, axis=0))
        block = jnp.concatenate(blocks, axis=1)
        here = pl.ds(first, xw)
        right_v[:, here] = block.astype(f32)
        update = dot(both, jnp.concatenate([block, block], axis=0))
        err_v[:, here] = (m_v[:, here] - update).astype(bf16)
        copies.append(pltpu.make_async_copy(err_v.at[:, here], err.at[:, here], sems.at[3 + k]))
        copies[-1].start()
    copies.append(pltpu.make_async_copy(right_v, right_out, sems.at[2]))
    copies[-1].start()
    for copy in copies:
        copy.wait()


def shards(cotangent, gate_pre, up_pre, down_weight, gate_weight, up_weight, error_in, factor_in):
    G = NX * NC
    rows, D = cotangent.shape
    half = rows // 2
    TOK = NY * rows
    F = down_weight.shape[0]
    RANK = factor_in.shape[1]
    hw = D // NC
    xw = hw // NX
    zw = xw // (NZ // 4)
    VM = pltpu.VMEM
    DMA = pltpu.SemaphoreType.DMA
    piece = RANK // NZ
    scratch = [
        VM((NY, rows, D), bf16), VM((F, D), bf16), VM((D, F), bf16), VM((D, F), bf16),
        VM((F, D), bf16), VM((RANK, D), f32), VM((2 * RANK, D), bf16),
        VM((TOK, F), bf16), VM((TOK, F), bf16), VM((TOK, F), bf16), VM((F, TOK), bf16),
        VM((NY, rows, RANK), f32), VM((RANK, F), f32), VM((TOK, F), bf16), VM((TOK, F), bf16),
        VM((NY, rows, D), bf16), VM((6, half, D), bf16), VM((2, half, D), bf16),
        VM((NZ, piece, F), f32), VM((NZ, piece, F), f32), VM((G, piece, F), f32), VM((NZ, piece, F), f32),
        VM((2 * RANK, F), bf16), VM((F, hw), bf16), VM((F, hw), bf16),
        VM((NX, F, xw), bf16), VM((NX, F, xw), bf16), VM((NZ, 16, zw), bf16), VM((NZ, 16, zw), bf16),
        DMA((8,)), DMA((6,)), DMA((6,)),
        DMA((NZ,)), DMA((NZ,)), DMA((G,)), DMA((G,)), DMA((NZ,)), DMA((NZ,)),
        DMA((1,)), DMA((1,)), DMA((NX,)), DMA((NX,)), DMA((NZ,)), DMA((NZ,)), DMA((NZ,)), DMA((NZ,)),
        DMA((NX,)), DMA((NX,)), DMA((NX,)), DMA((NX,)), DMA((6,)), DMA((6,)),
    ]
    in_vmem = pl.BlockSpec(memory_space=pltpu.VMEM)
    anywhere = pl.BlockSpec(memory_space=pl.ANY)
    held = pl.pallas_call(
        kernel,
        out_shape=(VM((rows, D), bf16), VM((RANK, F), f32), VM((NC, NX, NZ, 16, zw), bf16), VM((F, D), f32)),
        in_specs=[anywhere] * 8,
        out_specs=(in_vmem,) * 4,
        scratch_shapes=scratch,
        compiler_params=pltpu.CompilerParams(
            collective_id=0, has_side_effects=True, vmem_limit_bytes=VMEM_MIB * 1024 * 1024
        ),
        cost_estimate=pl.CostEstimate(flops=4 * 10**9, bytes_accessed=17 * 10**6, transcendentals=10**5),
    )(cotangent, gate_pre, up_pre, down_weight, gate_weight, up_weight, error_in[0], factor_in[0])
    shape = jax.ShapeDtypeStruct
    input_grad, left_t, right, error_out = pl.pallas_call(
        finish,
        out_shape=(shape((rows, D), bf16), shape((RANK, F), f32), shape((RANK, D), f32), shape((F, D), bf16)),
        in_specs=[in_vmem] * 4,
        out_specs=(anywhere,) * 4,
        scratch_shapes=[VM((RANK, D), f32), VM((F, D), bf16), DMA((3 + NC * NX,))],
        compiler_params=pltpu.CompilerParams(vmem_limit_bytes=16 * 1024 * 1024),
        cost_estimate=pl.CostEstimate(flops=3 * 10**8, bytes_accessed=9 * 10**6, transcendentals=0),
    )(*held)
    return (input_grad, left_t.T, right[None], error_out[None])


def solution(mesh):
    in_specs = (
        P(("dp", "tensor"), None),
        P("dp", "tensor"),
        P("dp", "tensor"),
        P("tensor", None),
        P(None, "tensor"),
        P(None, "tensor"),
        P("dp", "tensor", None),
        P("tensor", None, None),
    )
    out_specs = (
        P(("dp", "tensor"), None),
        P("tensor", None),
        P("tensor", None, None),
        P("dp", "tensor", None),
    )
    return jax.shard_map(shards, mesh=mesh, in_specs=in_specs, out_specs=out_specs, check_vma=False)
```

```python
import functools

import jax
import jax.numpy as jnp
from jax import lax
from jax.experimental import pallas as pl
from jax.experimental.pallas import tpu as pltpu
from jax.sharding import PartitionSpec as P

epsilon = 1e-06
NX, NZ, NC = 4, 8, 2
NY = 4
VMEM_MIB = 57
MESH = pl.DeviceIdType.MESH
f32, bf16 = jnp.float32, jnp.bfloat16
NN = (((1,), (0,)), ((), ()))
NT = (((1,), (1,)), ((), ()))


def dot(a, b, dims=NN):
    return lax.dot_general(a, b, dims, preferred_element_type=f32)


def split(a):
    high = a.astype(bf16)
    low = (a - high.astype(f32)).astype(bf16)
    return jnp.concatenate([high, low], axis=0)


def fold(a):
    half = a.shape[0] // 2
    return a[:half] + a[half:]


def kernel(
    c, gate, up, wd, wg, wu, e, f,
    ig_v, tt, rfull, m_v,
    cbuf, wd_v, wg_v, wu_v, e_v, f_v, fs, gate_v, up_v, hid, hid_t, y_v, pe, dg, du,
    part, ig_in, ig_sum,
    p1, p1_in, p2_in, t_v, ts, mc, mc_in, mx, mx_in, r2, r2_in,
    load, ag_s, ag_r, p1_s, p1_r, p2_s, p2_r, p3_s, p3_r,
    mc_s, mc_r, mx_s, mx_r, r2_s, r2_r, r3_s, r3_r, r4_s, r4_r, r5_s, r5_r, ig_s, ig_r,
):
    G = NX * NC
    rows, D = c.shape
    half = rows // 2
    TOK = NY * rows
    F = wd.shape[0]
    RANK = f.shape[0]
    hw = D // NC
    xw = hw // NX
    zw = xw // (NZ // 4)
    width = min(1024, hw)
    mean = 1.0 / (NX * NZ * NC)

    dp, y = lax.axis_index("dp"), lax.axis_index("tensor")
    core = lax.rem(dp, NC)
    z = lax.rem(dp // NC, NZ)
    x = dp // (NC * NZ)
    g = x * NC + core
    y_right, y_left, y_opp = (lax.rem(y + k, NY) for k in (1, 3, 2))

    def in_group(d):
        other = lax.rem(g + d, G)
        return (((other // NC) * NZ + z) * NC + lax.rem(other, NC), y)

    def in_x(d):
        return ((lax.rem(x + d, NX) * NZ + z) * NC + core, y)

    def in_z(d):
        return ((x * NZ + lax.rem(z + d, NZ)) * NC + core, y)

    sibling = (dp + 1 - 2 * core, y)

    z_far = sorted(range(1, NZ), key=lambda d: -min(d, NZ - d))
    x_far = sorted(range(1, NX), key=lambda d: -min(d, NX - d))
    g_far = sorted(range(1, G), key=lambda d: -min(d // NC, NX - d // NC))

    mine = cbuf.at[y]
    pairs = [(c, mine), (f, f_v), (e, e_v), (gate, gate_v), (up, up_v), (wd, wd_v), (wg, wg_v), (wu, wu_v)]
    loads = [pltpu.make_async_copy(a, b, load.at[k]) for k, (a, b) in enumerate(pairs)]
    for copy in loads:
        copy.start()

    barrier = pltpu.get_barrier_semaphore()
    partners = [(dp, y_right), (dp, y_left)]
    partners += [in_group(d) for d in range(1, G)] + [in_z(d) for d in range(1, NZ)]
    for other in partners:
        pl.semaphore_signal(barrier, inc=1, device_id=other, device_id_type=MESH)
    pl.semaphore_wait(barrier, len(partners))

    sent = []

    def send(src, dst, s, r, to):
        copy = pltpu.make_async_remote_copy(
            src_ref=src, dst_ref=dst, send_sem=s, recv_sem=r, device_id=to, device_id_type=MESH
        )
        copy.start()
        sent.append(copy)
        return copy

    right, left = (dp, y_right), (dp, y_left)
    A, B = pl.ds(0, half), pl.ds(half, half)

    def gather(k, src, dst, to):
        return send(src, dst, ag_s.at[k], ag_r.at[k], to)

    from_left_a = gather(0, c.at[A], cbuf.at[y, A], right)
    from_right_b = gather(1, c.at[B], cbuf.at[y, B], left)

    loads[1].wait()
    fs[...] = split(f_v[...])
    loads[0].wait()

    def tokens_times_factor(slot):
        both = dot(cbuf[slot], fs[...], NT)
        y_v[slot] = both[:, :RANK] + both[:, RANK:]

    tokens_times_factor(y)
    loads[2].wait()
    pe[...] = fold(dot(fs[...], e_v[...], NT))

    from_left_b = gather(2, c.at[B], cbuf.at[y, B], right)
    from_right_a = gather(3, c.at[A], cbuf.at[y, A], left)

    loads[3].wait()
    loads[4].wait()
    a, u = gate_v[...].astype(f32), up_v[...].astype(f32)
    hidden = a * jax.nn.sigmoid(a) * u
    hidden = hidden.astype(bf16).astype(f32)
    hid[...] = hidden.astype(bf16)
    hid_t[...] = hidden.T.astype(bf16)

    from_left_a.wait_recv()
    from_opp_a = gather(4, cbuf.at[y_left, A], cbuf.at[y_left, A], right)
    from_right_b.wait_recv()
    from_opp_b = gather(5, cbuf.at[y_right, B], cbuf.at[y_right, B], left)
    from_left_b.wait_recv()
    tokens_times_factor(y_left)
    from_right_a.wait_recv()
    tokens_times_factor(y_right)
    for k in (5, 6, 7):
        loads[k].wait()
    from_opp_a.wait_recv()
    from_opp_b.wait_recv()
    tokens_times_factor(y_opp)

    y_all = y_v[...].reshape(TOK, RANK)
    y_high = y_all.astype(bf16).astype(f32)
    y_both = jnp.concatenate([y_high, y_all - y_high], axis=1).T.astype(bf16)
    p_all = fold(dot(y_both, hid[...])) + pe[...]
    p1[...] = p_all.reshape(NZ, RANK // NZ, F)
    p1_copies = []
    for d in z_far:
        other = lax.rem(z + d, NZ)
        p1_copies.append(send(p1.at[other], p1_in.at[z], p1_s.at[d], p1_r.at[d], in_z(d)))
    p1_in[z] = p1[z]

    def weight_gradient(first, j):
        here = pl.ds(pl.multiple_of(first + j * width, width), width)
        block = cbuf[:, :, here].reshape(TOK, width)
        value = dot(hid_t[...], block) + e_v[:, here].astype(f32)
        m_v[:, here] = value
        return value

    for j in range(hw // width):
        mc[:, j * width : (j + 1) * width] = weight_gradient((1 - core) * hw, j).astype(bf16)
    mc_copy = send(mc, mc_in, mc_s.at[0], mc_r.at[0], sibling)
    for j in range(hw // width):
        weight_gradient(core * hw, j)

    grad = dot(cbuf[...].reshape(TOK, D), wd_v[...], NT)
    a, u = gate_v[...].astype(f32), up_v[...].astype(f32)
    s = jax.nn.sigmoid(a)
    dg[...] = (grad * u * s * (1.0 + a * (1.0 - s))).astype(bf16)
    du[...] = (grad * (a * s)).astype(bf16)
    def total_of(ref, count):
        total = ref[0].astype(f32)
        for k in range(1, count):
            total = total + ref[k].astype(f32)
        return total

    mc_copy.wait_recv()
    for k in range(NX):
        here = pl.ds(pl.multiple_of(core * hw + k * xw, xw), xw)
        mx[k] = (m_v[:, here] + mc_in[:, k * xw : (k + 1) * xw].astype(f32)).astype(bf16)

    for copy in p1_copies:
        copy.wait_recv()
    p2_in[g] = total_of(p1_in, NZ)
    p2_copies = [send(p2_in.at[g], p2_in.at[g], p2_s.at[d], p2_r.at[d], in_group(d)) for d in g_far]

    mx_copies = []
    for d in x_far:
        other = lax.rem(x + d, NX)
        mx_copies.append(send(mx.at[other], mx_in.at[x], mx_s.at[d], mx_r.at[d], in_x(d)))

    for j in range(D // width):
        here = pl.ds(j * width, width)
        value = dot(dg[...], wg_v[here, :], NT) + dot(du[...], wu_v[here, :], NT)
        part[:, :, here] = value.astype(bf16).reshape(NY, rows, width)

    def give(k, src, to):
        return send(src, ig_in.at[k], ig_s.at[k], ig_r.at[k], to)

    ig0 = give(0, part.at[y_opp, A], right)
    ig3 = give(3, part.at[y_opp, B], left)
    ig1 = give(1, part.at[y_right, B], right)
    ig4 = give(4, part.at[y_left, A], left)
    mx_in[x] = mx[x]

    for copy in p2_copies:
        copy.wait_recv()
    t_v[z] = total_of(p2_in, G)
    p3_copies = [send(t_v.at[z], t_v.at[z], p3_s.at[d], p3_r.at[d], in_z(d)) for d in z_far]
    for copy in p3_copies:
        copy.wait_recv()

    row_ids = lax.broadcasted_iota(jnp.int32, (RANK, 1), 0)
    tt[...] = t_v[...].reshape(RANK, F) * mean

    def column(k, carry):
        vector = tt[pl.ds(k, 1), :]
        tile = tt[...]
        squares = jnp.sum(vector * vector, axis=1, keepdims=True) + epsilon
        factors = jnp.sum(tile * vector, axis=1, keepdims=True) * (1.0 / squares)
        tt[...] = tile - jnp.where(row_ids > k, factors, 0.0) * vector
        tt[pl.ds(k, 1), :] = vector * lax.rsqrt(squares)
        return carry

    lax.fori_loop(0, RANK, column, 0)
    ts[...] = split(tt[...])

    for copy in mx_copies:
        copy.wait_recv()
    m_sum = total_of(mx_in, NX)
    m_high = m_sum.astype(bf16)
    m_low = (m_sum - m_high.astype(f32)).astype(bf16)
    r_all = fold(dot(ts[...], m_high)) + dot(ts[:RANK], m_low)
    for k in range(NZ):
        q, h = k % 4, k // 4
        r2[k] = r_all[16 * q : 16 * q + 16, h * zw : (h + 1) * zw].astype(bf16)
    r2_copies = []
    for d in z_far:
        other = lax.rem(z + d, NZ)
        r2_copies.append(send(r2.at[other], r2_in.at[z], r2_s.at[d], r2_r.at[d], in_z(d)))
    r2_in[z] = r2[z]

    ig0.wait_recv()
    ig_sum[0] = (ig_in[0].astype(f32) + part[y_right, A].astype(f32)).astype(bf16)
    ig2 = give(2, ig_sum.at[0], right)
    ig3.wait_recv()
    ig_sum[1] = (ig_in[3].astype(f32) + part[y_left, B].astype(f32)).astype(bf16)
    ig5 = give(5, ig_sum.at[1], left)

    def all_left():
        for copy in sent:
            copy.wait_send()
        sent.clear()

    all_left()
    for copy in r2_copies:
        copy.wait_recv()
    rfull[core, x, z] = (total_of(r2_in, NZ) * mean).astype(bf16)
    own = rfull.at[core, x, z]
    r3_copies = {d: send(own, own, r3_s.at[d], r3_r.at[d], in_z(d)) for d in z_far}

    r4_copies = {}

    def along_x(k):
        piece = rfull.at[core, x, lax.rem(z + NZ - k, NZ)]
        for d in x_far:
            r4_copies[d, k] = send(piece, piece, r4_s.at[d, k], r4_r.at[d, k], in_x(d))

    along_x(0)
    for k in reversed(z_far):
        r3_copies[k].wait_recv()
        along_x(k)
    own = rfull.at[core, x]
    r5_copies = [send(own, own, r5_s.at[0], r5_r.at[0], sibling)]

    ig1.wait_recv()
    ig4.wait_recv()
    ig2.wait_recv()
    own_a = part[y, A].astype(f32) + ig_in[2].astype(f32) + ig_in[4].astype(f32)
    ig_v[A] = own_a.astype(bf16)
    ig5.wait_recv()
    own_b = part[y, B].astype(f32) + ig_in[1].astype(f32) + ig_in[5].astype(f32)
    ig_v[B] = own_b.astype(bf16)

    for d in reversed(x_far):
        for k in range(NZ):
            r4_copies[d, k].wait_recv()
        came = rfull.at[core, lax.rem(x + NX - d, NX)]
        r5_copies.append(send(came, came, r5_s.at[d], r5_r.at[d], sibling))
    for copy in r5_copies:
        copy.wait_recv()
    all_left()


def finish(ig_v, tt, rfull, m_v, ig, left_out, right_out, err, right_v, err_v, sems):
    RANK, F = tt.shape
    D = m_v.shape[1]
    hw = D // NC
    xw = hw // NX
    zw = xw // (NZ // 4)
    copies = [
        pltpu.make_async_copy(ig_v, ig, sems.at[0]),
        pltpu.make_async_copy(tt, left_out, sems.at[1]),
    ]
    for copy in copies:
        copy.start()
    high = tt[...].astype(bf16).astype(f32)
    both = jnp.concatenate([high, tt[...] - high], axis=0).T.astype(bf16)
    for k in range(NC * NX):
        first = k * xw
        blocks = []
        for h in range(NZ // 4):
            rows = [rfull[k // NX, k % NX, 4 * h + q] for q in range(4)]
            blocks.append(jnp.concatenate(rows, axis=0))
        block = jnp.concatenate(blocks, axis=1)
        here = pl.ds(first, xw)
        right_v[:, here] = block.astype(f32)
        update = dot(both, jnp.concatenate([block, block], axis=0))
        err_v[:, here] = (m_v[:, here] - update).astype(bf16)
        copies.append(pltpu.make_async_copy(err_v.at[:, here], err.at[:, here], sems.at[3 + k]))
        copies[-1].start()
    copies.append(pltpu.make_async_copy(right_v, right_out, sems.at[2]))
    copies[-1].start()
    for copy in copies:
        copy.wait()


def shards(cotangent, gate_pre, up_pre, down_weight, gate_weight, up_weight, error_in, factor_in):
    G = NX * NC
    rows, D = cotangent.shape
    half = rows // 2
    TOK = NY * rows
    F = down_weight.shape[0]
    RANK = factor_in.shape[1]
    hw = D // NC
    xw = hw // NX
    zw = xw // (NZ // 4)
    VM = pltpu.VMEM
    DMA = pltpu.SemaphoreType.DMA
    piece = RANK // NZ
    scratch = [
        VM((NY, rows, D), bf16), VM((F, D), bf16), VM((D, F), bf16), VM((D, F), bf16),
        VM((F, D), bf16), VM((RANK, D), f32), VM((2 * RANK, D), bf16),
        VM((TOK, F), bf16), VM((TOK, F), bf16), VM((TOK, F), bf16), VM((F, TOK), bf16),
        VM((NY, rows, RANK), f32), VM((RANK, F), f32), VM((TOK, F), bf16), VM((TOK, F), bf16),
        VM((NY, rows, D), bf16), VM((6, half, D), bf16), VM((2, half, D), bf16),
        VM((NZ, piece, F), f32), VM((NZ, piece, F), f32), VM((G, piece, F), f32), VM((NZ, piece, F), f32),
        VM((2 * RANK, F), bf16), VM((F, hw), bf16), VM((F, hw), bf16),
        VM((NX, F, xw), bf16), VM((NX, F, xw), bf16), VM((NZ, 16, zw), bf16), VM((NZ, 16, zw), bf16),
        DMA((8,)), DMA((6,)), DMA((6,)),
        DMA((NZ,)), DMA((NZ,)), DMA((G,)), DMA((G,)), DMA((NZ,)), DMA((NZ,)),
        DMA((1,)), DMA((1,)), DMA((NX,)), DMA((NX,)), DMA((NZ,)), DMA((NZ,)), DMA((NZ,)), DMA((NZ,)),
        DMA((NX, NZ)), DMA((NX, NZ)), DMA((NX,)), DMA((NX,)), DMA((6,)), DMA((6,)),
    ]
    in_vmem = pl.BlockSpec(memory_space=pltpu.VMEM)
    anywhere = pl.BlockSpec(memory_space=pl.ANY)
    held = pl.pallas_call(
        kernel,
        out_shape=(VM((rows, D), bf16), VM((RANK, F), f32), VM((NC, NX, NZ, 16, zw), bf16), VM((F, D), f32)),
        in_specs=[anywhere] * 8,
        out_specs=(in_vmem,) * 4,
        scratch_shapes=scratch,
        compiler_params=pltpu.CompilerParams(
            collective_id=0, has_side_effects=True, vmem_limit_bytes=VMEM_MIB * 1024 * 1024
        ),
        cost_estimate=pl.CostEstimate(flops=4 * 10**9, bytes_accessed=17 * 10**6, transcendentals=10**5),
    )(cotangent, gate_pre, up_pre, down_weight, gate_weight, up_weight, error_in[0], factor_in[0])
    shape = jax.ShapeDtypeStruct
    input_grad, left_t, right, error_out = pl.pallas_call(
        finish,
        out_shape=(shape((rows, D), bf16), shape((RANK, F), f32), shape((RANK, D), f32), shape((F, D), bf16)),
        in_specs=[in_vmem] * 4,
        out_specs=(anywhere,) * 4,
        scratch_shapes=[VM((RANK, D), f32), VM((F, D), bf16), DMA((3 + NC * NX,))],
        compiler_params=pltpu.CompilerParams(vmem_limit_bytes=16 * 1024 * 1024),
        cost_estimate=pl.CostEstimate(flops=3 * 10**8, bytes_accessed=9 * 10**6, transcendentals=0),
    )(*held)
    return (input_grad, left_t.T, right[None], error_out[None])


def solution(mesh):
    in_specs = (
        P(("dp", "tensor"), None),
        P("dp", "tensor"),
        P("dp", "tensor"),
        P("tensor", None),
        P(None, "tensor"),
        P(None, "tensor"),
        P("dp", "tensor", None),
        P("tensor", None, None),
    )
    out_specs = (
        P(("dp", "tensor"), None),
        P("tensor", None),
        P("tensor", None, None),
        P("dp", "tensor", None),
    )
    return jax.shard_map(shards, mesh=mesh, in_specs=in_specs, out_specs=out_specs, check_vma=False)
```

```python
import functools

import jax
import jax.numpy as jnp
from jax import lax
from jax.experimental import pallas as pl
from jax.experimental.pallas import tpu as pltpu
from jax.sharding import PartitionSpec as P

epsilon = 1e-06
NX, NZ, NC = 4, 8, 2
NY = 4
VMEM_MIB = 57
NQ = 4
MESH = pl.DeviceIdType.MESH
f32, bf16 = jnp.float32, jnp.bfloat16
NN = (((1,), (0,)), ((), ()))
NT = (((1,), (1,)), ((), ()))


def dot(a, b, dims=NN):
    return lax.dot_general(a, b, dims, preferred_element_type=f32)


def split(a):
    high = a.astype(bf16)
    low = (a - high.astype(f32)).astype(bf16)
    return jnp.concatenate([high, low], axis=0)


def fold(a):
    half = a.shape[0] // 2
    return a[:half] + a[half:]


def kernel(
    c, gate, up, wd, wg, wu, e, f,
    ig_v, tt, rfull, m_v,
    cbuf, wd_v, wg_v, wu_v, e_v, f_v, fs, gate_v, up_v, hid, hid_t, y_v, pe, dg, du,
    part, ig_in, ig_sum,
    p1, p1_in, p2_in, t_v, ts, mc, mc_in, mx, mx_in, r2, r2_in,
    load, ag_s, ag_r, p1_s, p1_r, p2_s, p2_r, p3_s, p3_r,
    mc_s, mc_r, mx_s, mx_r, r2_s, r2_r, r3_s, r3_r, r4_s, r4_r, r5_s, r5_r, ig_s, ig_r,
):
    G = NX * NC
    rows, D = c.shape
    half = rows // 2
    TOK = NY * rows
    F = wd.shape[0]
    RANK = f.shape[0]
    hw = D // NC
    qw = hw // NQ
    pw = qw // NX
    zw = NQ * pw // (NZ // 4)
    width = min(1024, hw)
    mean = 1.0 / (NX * NZ * NC)

    dp, y = lax.axis_index("dp"), lax.axis_index("tensor")
    core = lax.rem(dp, NC)
    z = lax.rem(dp // NC, NZ)
    x = dp // (NC * NZ)
    g = x * NC + core
    y_right, y_left, y_opp = (lax.rem(y + k, NY) for k in (1, 3, 2))

    def in_group(d):
        other = lax.rem(g + d, G)
        return (((other // NC) * NZ + z) * NC + lax.rem(other, NC), y)

    def in_x(d):
        return ((lax.rem(x + d, NX) * NZ + z) * NC + core, y)

    def in_z(d):
        return ((x * NZ + lax.rem(z + d, NZ)) * NC + core, y)

    sibling = (dp + 1 - 2 * core, y)

    z_far = sorted(range(1, NZ), key=lambda d: -min(d, NZ - d))
    x_far = sorted(range(1, NX), key=lambda d: -min(d, NX - d))
    g_far = sorted(range(1, G), key=lambda d: -min(d // NC, NX - d // NC))

    mine = cbuf.at[y]
    pairs = [(c, mine), (f, f_v), (e, e_v), (gate, gate_v), (up, up_v), (wd, wd_v), (wg, wg_v), (wu, wu_v)]
    loads = [pltpu.make_async_copy(a, b, load.at[k]) for k, (a, b) in enumerate(pairs)]
    for copy in loads:
        copy.start()

    barrier = pltpu.get_barrier_semaphore()
    partners = [(dp, y_right), (dp, y_left)]
    partners += [in_group(d) for d in range(1, G)] + [in_z(d) for d in range(1, NZ)]
    for other in partners:
        pl.semaphore_signal(barrier, inc=1, device_id=other, device_id_type=MESH)
    pl.semaphore_wait(barrier, len(partners))

    sent = []

    def send(src, dst, s, r, to):
        copy = pltpu.make_async_remote_copy(
            src_ref=src, dst_ref=dst, send_sem=s, recv_sem=r, device_id=to, device_id_type=MESH
        )
        copy.start()
        sent.append(copy)
        return copy

    right, left = (dp, y_right), (dp, y_left)
    A, B = pl.ds(0, half), pl.ds(half, half)

    def gather(k, src, dst, to):
        return send(src, dst, ag_s.at[k], ag_r.at[k], to)

    from_left_a = gather(0, c.at[A], cbuf.at[y, A], right)
    from_right_b = gather(1, c.at[B], cbuf.at[y, B], left)

    loads[1].wait()
    fs[...] = split(f_v[...])
    loads[0].wait()

    def tokens_times_factor(slot):
        both = dot(cbuf[slot], fs[...], NT)
        y_v[slot] = both[:, :RANK] + both[:, RANK:]

    tokens_times_factor(y)
    loads[2].wait()
    pe[...] = fold(dot(fs[...], e_v[...], NT))

    from_left_b = gather(2, c.at[B], cbuf.at[y, B], right)
    from_right_a = gather(3, c.at[A], cbuf.at[y, A], left)

    loads[3].wait()
    loads[4].wait()
    a, u = gate_v[...].astype(f32), up_v[...].astype(f32)
    hidden = a * jax.nn.sigmoid(a) * u
    hidden = hidden.astype(bf16).astype(f32)
    hid[...] = hidden.astype(bf16)
    hid_t[...] = hidden.T.astype(bf16)

    from_left_a.wait_recv()
    from_opp_a = gather(4, cbuf.at[y_left, A], cbuf.at[y_left, A], right)
    from_right_b.wait_recv()
    from_opp_b = gather(5, cbuf.at[y_right, B], cbuf.at[y_right, B], left)
    from_left_b.wait_recv()
    tokens_times_factor(y_left)
    from_right_a.wait_recv()
    tokens_times_factor(y_right)
    for k in (5, 6, 7):
        loads[k].wait()
    from_opp_a.wait_recv()
    from_opp_b.wait_recv()
    tokens_times_factor(y_opp)

    y_all = y_v[...].reshape(TOK, RANK)
    y_high = y_all.astype(bf16).astype(f32)
    y_both = jnp.concatenate([y_high, y_all - y_high], axis=1).T.astype(bf16)
    p_all = fold(dot(y_both, hid[...])) + pe[...]
    p1[...] = p_all.reshape(NZ, RANK // NZ, F)
    p1_copies = []
    for d in z_far:
        other = lax.rem(z + d, NZ)
        p1_copies.append(send(p1.at[other], p1_in.at[z], p1_s.at[d], p1_r.at[d], in_z(d)))
    p1_in[z] = p1[z]

    def weight_gradient(first):
        here = pl.ds(pl.multiple_of(first, qw), qw)
        block = cbuf[:, :, here].reshape(TOK, qw)
        value = dot(hid_t[...], block) + e_v[:, here].astype(f32)
        m_v[:, here] = value
        return value

    rest = pl.ds(1, NQ - 1)
    mc[0] = weight_gradient((1 - core) * hw).astype(bf16)
    mc_first = send(mc.at[0], mc_in.at[0], mc_s.at[0], mc_r.at[0], sibling)
    for q in range(1, NQ):
        mc[q] = weight_gradient((1 - core) * hw + q * qw).astype(bf16)
    mc_rest = send(mc.at[rest], mc_in.at[rest], mc_s.at[1], mc_r.at[1], sibling)
    for q in range(NQ):
        weight_gradient(core * hw + q * qw)

    def chip_sum(q):
        for k in range(NX):
            here = pl.ds(pl.multiple_of(core * hw + q * qw + k * pw, pw), pw)
            mx[k, q] = (m_v[:, here] + mc_in[q, :, k * pw : (k + 1) * pw].astype(f32)).astype(bf16)

    grad = dot(cbuf[...].reshape(TOK, D), wd_v[...], NT)
    mc_first.wait_recv()
    chip_sum(0)
    mx_first, mx_rest = [], []
    for d in x_far:
        other = lax.rem(x + d, NX)
        mx_first.append(send(mx.at[other, 0], mx_in.at[x, 0], mx_s.at[0, d], mx_r.at[0, d], in_x(d)))
    a, u = gate_v[...].astype(f32), up_v[...].astype(f32)
    s = jax.nn.sigmoid(a)
    dg[...] = (grad * u * s * (1.0 + a * (1.0 - s))).astype(bf16)
    du[...] = (grad * (a * s)).astype(bf16)

    def part_tile(j):
        here = pl.ds(j * width, width)
        value = dot(dg[...], wg_v[here, :], NT) + dot(du[...], wu_v[here, :], NT)
        part[:, :, here] = value.astype(bf16).reshape(NY, rows, width)

    tiles = D // width
    for j in range(tiles // 2):
        part_tile(j)

    def give(k, src, to):
        return send(src, ig_in.at[k], ig_s.at[k], ig_r.at[k], to)

    def total_of(ref, count):
        total = ref[0].astype(f32)
        for k in range(1, count):
            total = total + ref[k].astype(f32)
        return total

    for copy in p1_copies:
        copy.wait_recv()
    p2_in[g] = total_of(p1_in, NZ)
    p2_copies = [send(p2_in.at[g], p2_in.at[g], p2_s.at[d], p2_r.at[d], in_group(d)) for d in g_far]

    mc_rest.wait_recv()
    for q in range(1, NQ):
        chip_sum(q)
    for j in range(tiles // 2, tiles):
        part_tile(j)
    ig0 = give(0, part.at[y_opp, A], right)
    ig3 = give(3, part.at[y_opp, B], left)
    ig1 = give(1, part.at[y_right, B], right)
    ig4 = give(4, part.at[y_left, A], left)
    for copy in p2_copies:
        copy.wait_recv()
    t_v[z] = total_of(p2_in, G)
    p3_copies = [send(t_v.at[z], t_v.at[z], p3_s.at[d], p3_r.at[d], in_z(d)) for d in z_far]
    for d in x_far:
        other = lax.rem(x + d, NX)
        src, dst = mx.at[other, rest], mx_in.at[x, rest]
        mx_rest.append(send(src, dst, mx_s.at[1, d], mx_r.at[1, d], in_x(d)))
    mx_in[x] = mx[x]
    for copy in p3_copies:
        copy.wait_recv()

    row_ids = lax.broadcasted_iota(jnp.int32, (RANK, 1), 0)
    tt[...] = t_v[...].reshape(RANK, F) * mean

    def column(k, carry):
        vector = tt[pl.ds(k, 1), :]
        tile = tt[...]
        squares = jnp.sum(vector * vector, axis=1, keepdims=True) + epsilon
        factors = jnp.sum(tile * vector, axis=1, keepdims=True) * (1.0 / squares)
        tt[...] = tile - jnp.where(row_ids > k, factors, 0.0) * vector
        tt[pl.ds(k, 1), :] = vector * lax.rsqrt(squares)
        return carry

    lax.fori_loop(0, RANK, column, 0)
    ts[...] = split(tt[...])

    for copy in mx_first + mx_rest:
        copy.wait_recv()
    m_sum = total_of(mx_in, NX)
    m_sum = jnp.concatenate([m_sum[q] for q in range(NQ)], axis=1)
    m_high = m_sum.astype(bf16)
    m_low = (m_sum - m_high.astype(f32)).astype(bf16)
    r_all = fold(dot(ts[...], m_high)) + dot(ts[:RANK], m_low)
    for k in range(NZ):
        q, h = k % 4, k // 4
        r2[k] = r_all[16 * q : 16 * q + 16, h * zw : (h + 1) * zw].astype(bf16)
    r2_copies = []
    for d in z_far:
        other = lax.rem(z + d, NZ)
        r2_copies.append(send(r2.at[other], r2_in.at[z], r2_s.at[d], r2_r.at[d], in_z(d)))
    r2_in[z] = r2[z]

    ig0.wait_recv()
    ig_sum[0] = (ig_in[0].astype(f32) + part[y_right, A].astype(f32)).astype(bf16)
    ig2 = give(2, ig_sum.at[0], right)
    ig3.wait_recv()
    ig_sum[1] = (ig_in[3].astype(f32) + part[y_left, B].astype(f32)).astype(bf16)
    ig5 = give(5, ig_sum.at[1], left)

    def all_left():
        for copy in sent:
            copy.wait_send()
        sent.clear()

    all_left()
    for copy in r2_copies:
        copy.wait_recv()
    rfull[core, x, z] = (total_of(r2_in, NZ) * mean).astype(bf16)
    own = rfull.at[core, x, z]
    r3_copies = {d: send(own, own, r3_s.at[d], r3_r.at[d], in_z(d)) for d in z_far}

    r4_copies = {}

    def along_x(k):
        piece = rfull.at[core, x, lax.rem(z + NZ - k, NZ)]
        for d in x_far:
            r4_copies[d, k] = send(piece, piece, r4_s.at[d, k], r4_r.at[d, k], in_x(d))

    along_x(0)
    for k in reversed(z_far):
        r3_copies[k].wait_recv()
        along_x(k)
    own = rfull.at[core, x]
    r5_copies = [send(own, own, r5_s.at[0], r5_r.at[0], sibling)]

    ig1.wait_recv()
    ig4.wait_recv()
    ig2.wait_recv()
    own_a = part[y, A].astype(f32) + ig_in[2].astype(f32) + ig_in[4].astype(f32)
    ig_v[A] = own_a.astype(bf16)
    ig5.wait_recv()
    own_b = part[y, B].astype(f32) + ig_in[1].astype(f32) + ig_in[5].astype(f32)
    ig_v[B] = own_b.astype(bf16)

    for d in reversed(x_far):
        for k in range(NZ):
            r4_copies[d, k].wait_recv()
        came = rfull.at[core, lax.rem(x + NX - d, NX)]
        r5_copies.append(send(came, came, r5_s.at[d], r5_r.at[d], sibling))
    for copy in r5_copies:
        copy.wait_recv()
    all_left()


def finish(ig_v, tt, rfull, m_v, ig, left_out, right_out, err, right_v, err_v, sems):
    RANK, F = tt.shape
    D = m_v.shape[1]
    hw = D // NC
    qw = hw // NQ
    pw = qw // NX
    zw = NQ * pw // (NZ // 4)
    copies = [
        pltpu.make_async_copy(ig_v, ig, sems.at[0]),
        pltpu.make_async_copy(tt, left_out, sems.at[1]),
    ]
    for copy in copies:
        copy.start()
    high = tt[...].astype(bf16).astype(f32)
    both = jnp.concatenate([high, tt[...] - high], axis=0).T.astype(bf16)
    for k in range(NC * NQ):
        h, at = divmod(k % NQ * pw, zw)
        blocks = []
        for chip in range(NX):
            rows = [rfull[k // NQ, chip, 4 * h + q, :, at : at + pw] for q in range(4)]
            blocks.append(jnp.concatenate(rows, axis=0))
        block = jnp.concatenate(blocks, axis=1)
        here = pl.ds(k * qw, qw)
        right_v[:, here] = block.astype(f32)
        update = dot(both, jnp.concatenate([block, block], axis=0))
        err_v[:, here] = (m_v[:, here] - update).astype(bf16)
        copies.append(pltpu.make_async_copy(err_v.at[:, here], err.at[:, here], sems.at[3 + k]))
        copies[-1].start()
    copies.append(pltpu.make_async_copy(right_v, right_out, sems.at[2]))
    copies[-1].start()
    for copy in copies:
        copy.wait()


def shards(cotangent, gate_pre, up_pre, down_weight, gate_weight, up_weight, error_in, factor_in):
    G = NX * NC
    rows, D = cotangent.shape
    half = rows // 2
    TOK = NY * rows
    F = down_weight.shape[0]
    RANK = factor_in.shape[1]
    hw = D // NC
    qw = hw // NQ
    pw = qw // NX
    zw = NQ * pw // (NZ // 4)
    VM = pltpu.VMEM
    DMA = pltpu.SemaphoreType.DMA
    piece = RANK // NZ
    scratch = [
        VM((NY, rows, D), bf16), VM((F, D), bf16), VM((D, F), bf16), VM((D, F), bf16),
        VM((F, D), bf16), VM((RANK, D), f32), VM((2 * RANK, D), bf16),
        VM((TOK, F), bf16), VM((TOK, F), bf16), VM((TOK, F), bf16), VM((F, TOK), bf16),
        VM((NY, rows, RANK), f32), VM((RANK, F), f32), VM((TOK, F), bf16), VM((TOK, F), bf16),
        VM((NY, rows, D), bf16), VM((6, half, D), bf16), VM((2, half, D), bf16),
        VM((NZ, piece, F), f32), VM((NZ, piece, F), f32), VM((G, piece, F), f32), VM((NZ, piece, F), f32),
        VM((2 * RANK, F), bf16), VM((NQ, F, qw), bf16), VM((NQ, F, qw), bf16),
        VM((NX, NQ, F, pw), bf16), VM((NX, NQ, F, pw), bf16), VM((NZ, 16, zw), bf16), VM((NZ, 16, zw), bf16),
        DMA((8,)), DMA((6,)), DMA((6,)),
        DMA((NZ,)), DMA((NZ,)), DMA((G,)), DMA((G,)), DMA((NZ,)), DMA((NZ,)),
        DMA((2,)), DMA((2,)), DMA((2, NX)), DMA((2, NX)), DMA((NZ,)), DMA((NZ,)), DMA((NZ,)), DMA((NZ,)),
        DMA((NX, NZ)), DMA((NX, NZ)), DMA((NX,)), DMA((NX,)), DMA((6,)), DMA((6,)),
    ]
    in_vmem = pl.BlockSpec(memory_space=pltpu.VMEM)
    anywhere = pl.BlockSpec(memory_space=pl.ANY)
    held = pl.pallas_call(
        kernel,
        out_shape=(VM((rows, D), bf16), VM((RANK, F), f32), VM((NC, NX, NZ, 16, zw), bf16), VM((F, D), f32)),
        in_specs=[anywhere] * 8,
        out_specs=(in_vmem,) * 4,
        scratch_shapes=scratch,
        compiler_params=pltpu.CompilerParams(
            collective_id=0, has_side_effects=True, vmem_limit_bytes=VMEM_MIB * 1024 * 1024
        ),
        cost_estimate=pl.CostEstimate(flops=4 * 10**9, bytes_accessed=17 * 10**6, transcendentals=10**5),
    )(cotangent, gate_pre, up_pre, down_weight, gate_weight, up_weight, error_in[0], factor_in[0])
    shape = jax.ShapeDtypeStruct
    input_grad, left_t, right, error_out = pl.pallas_call(
        finish,
        out_shape=(shape((rows, D), bf16), shape((RANK, F), f32), shape((RANK, D), f32), shape((F, D), bf16)),
        in_specs=[in_vmem] * 4,
        out_specs=(anywhere,) * 4,
        scratch_shapes=[VM((RANK, D), f32), VM((F, D), bf16), DMA((3 + NC * NQ,))],
        compiler_params=pltpu.CompilerParams(vmem_limit_bytes=16 * 1024 * 1024),
        cost_estimate=pl.CostEstimate(flops=3 * 10**8, bytes_accessed=9 * 10**6, transcendentals=0),
    )(*held)
    return (input_grad, left_t.T, right[None], error_out[None])


def solution(mesh):
    in_specs = (
        P(("dp", "tensor"), None),
        P("dp", "tensor"),
        P("dp", "tensor"),
        P("tensor", None),
        P(None, "tensor"),
        P(None, "tensor"),
        P("dp", "tensor", None),
        P("tensor", None, None),
    )
    out_specs = (
        P(("dp", "tensor"), None),
        P("tensor", None),
        P("tensor", None, None),
        P("dp", "tensor", None),
    )
    return jax.shard_map(shards, mesh=mesh, in_specs=in_specs, out_specs=out_specs, check_vma=False)
```

```python
import functools

import jax
import jax.numpy as jnp
from jax import lax
from jax.experimental import pallas as pl
from jax.experimental.pallas import tpu as pltpu
from jax.sharding import PartitionSpec as P

epsilon = 1e-06
NX, NZ, NC = 4, 8, 2
NY = 4
VMEM_MIB = 57
NQ = 4
MESH = pl.DeviceIdType.MESH
f32, bf16 = jnp.float32, jnp.bfloat16
NN = (((1,), (0,)), ((), ()))
NT = (((1,), (1,)), ((), ()))


def dot(a, b, dims=NN):
    return lax.dot_general(a, b, dims, preferred_element_type=f32)


def split(a):
    high = a.astype(bf16)
    low = (a - high.astype(f32)).astype(bf16)
    return jnp.concatenate([high, low], axis=0)


def fold(a):
    half = a.shape[0] // 2
    return a[:half] + a[half:]


def kernel(
    c, gate, up, wd, wg, wu, e, f,
    ig_v, tt, rfull, m_v,
    cbuf, wd_v, wg_v, wu_v, e_v, f_v, fs, gate_v, up_v, hid, hid_t, y_v, pe, dg, du,
    part, ig_in, ig_sum,
    p1, p1_in, p2_in, t_v, ts, mc, mc_in, mx, mx_in, r2, r2_in,
    load, ag_s, ag_r, p1_s, p1_r, p2_s, p2_r, p3_s, p3_r,
    mc_s, mc_r, mx_s, mx_r, r2_s, r2_r, r3_s, r3_r, r4_s, r4_r, r5_s, r5_r, ig_s, ig_r,
):
    G = NX * NC
    rows, D = c.shape
    half = rows // 2
    TOK = NY * rows
    F = wd.shape[0]
    RANK = f.shape[0]
    hw = D // NC
    qw = hw // NQ
    pw = qw // NX
    zw = NQ * pw // (NZ // 4)
    width = min(1024, hw)
    mean = 1.0 / (NX * NZ * NC)

    dp, y = lax.axis_index("dp"), lax.axis_index("tensor")
    core = lax.rem(dp, NC)
    z = lax.rem(dp // NC, NZ)
    x = dp // (NC * NZ)
    g = x * NC + core
    y_right, y_left, y_opp = (lax.rem(y + k, NY) for k in (1, 3, 2))

    def in_group(d):
        other = lax.rem(g + d, G)
        return (((other // NC) * NZ + z) * NC + lax.rem(other, NC), y)

    def in_x(d):
        return ((lax.rem(x + d, NX) * NZ + z) * NC + core, y)

    def in_z(d):
        return ((x * NZ + lax.rem(z + d, NZ)) * NC + core, y)

    sibling = (dp + 1 - 2 * core, y)

    z_far = sorted(range(1, NZ), key=lambda d: -min(d, NZ - d))
    x_far = sorted(range(1, NX), key=lambda d: -min(d, NX - d))
    g_far = sorted(range(1, G), key=lambda d: -min(d // NC, NX - d // NC))

    mine = cbuf.at[y]
    pairs = [(c, mine), (f, f_v), (e, e_v), (gate, gate_v), (up, up_v), (wd, wd_v), (wg, wg_v), (wu, wu_v)]
    loads = [pltpu.make_async_copy(a, b, load.at[k]) for k, (a, b) in enumerate(pairs)]
    for copy in loads:
        copy.start()

    barrier = pltpu.get_barrier_semaphore()
    partners = [(dp, y_right), (dp, y_left)]
    partners += [in_group(d) for d in range(1, G)] + [in_z(d) for d in range(1, NZ)]
    for other in partners:
        pl.semaphore_signal(barrier, inc=1, device_id=other, device_id_type=MESH)
    pl.semaphore_wait(barrier, len(partners))

    sent = []

    def send(src, dst, s, r, to):
        copy = pltpu.make_async_remote_copy(
            src_ref=src, dst_ref=dst, send_sem=s, recv_sem=r, device_id=to, device_id_type=MESH
        )
        copy.start()
        sent.append(copy)
        return copy

    right, left = (dp, y_right), (dp, y_left)
    A, B = pl.ds(0, half), pl.ds(half, half)

    def gather(k, src, dst, to):
        return send(src, dst, ag_s.at[k], ag_r.at[k], to)

    from_left_a = gather(0, c.at[A], cbuf.at[y, A], right)
    from_right_b = gather(1, c.at[B], cbuf.at[y, B], left)

    loads[1].wait()
    fs[...] = split(f_v[...])
    loads[0].wait()

    def tokens_times_factor(slot):
        both = dot(cbuf[slot], fs[...], NT)
        y_v[slot] = both[:, :RANK] + both[:, RANK:]

    tokens_times_factor(y)
    loads[2].wait()
    pe[...] = fold(dot(fs[...], e_v[...], NT))

    from_left_b = gather(2, c.at[B], cbuf.at[y, B], right)
    from_right_a = gather(3, c.at[A], cbuf.at[y, A], left)

    loads[3].wait()
    loads[4].wait()
    a, u = gate_v[...].astype(f32), up_v[...].astype(f32)
    hidden = a * jax.nn.sigmoid(a) * u
    hidden = hidden.astype(bf16).astype(f32)
    hid[...] = hidden.astype(bf16)
    hid_t[...] = hidden.T.astype(bf16)

    from_left_a.wait_recv()
    from_opp_a = gather(4, cbuf.at[y_left, A], cbuf.at[y_left, A], right)
    from_right_b.wait_recv()
    from_opp_b = gather(5, cbuf.at[y_right, B], cbuf.at[y_right, B], left)
    from_left_b.wait_recv()
    tokens_times_factor(y_left)
    from_right_a.wait_recv()
    tokens_times_factor(y_right)
    for k in (5, 6, 7):
        loads[k].wait()
    from_opp_a.wait_recv()
    from_opp_b.wait_recv()
    tokens_times_factor(y_opp)

    y_all = y_v[...].reshape(TOK, RANK)
    y_high = y_all.astype(bf16).astype(f32)
    y_both = jnp.concatenate([y_high, y_all - y_high], axis=1).T.astype(bf16)
    p_all = fold(dot(y_both, hid[...])) + pe[...]
    p1[...] = p_all.reshape(NZ, RANK // NZ, F)
    p1_copies = []
    for d in z_far:
        other = lax.rem(z + d, NZ)
        p1_copies.append(send(p1.at[other], p1_in.at[z], p1_s.at[d], p1_r.at[d], in_z(d)))
    p1_in[z] = p1[z]

    def weight_gradient(first):
        here = pl.ds(pl.multiple_of(first, qw), qw)
        block = cbuf[:, :, here].reshape(TOK, qw)
        value = dot(hid_t[...], block) + e_v[:, here].astype(f32)
        m_v[:, here] = value
        return value

    rest = pl.ds(1, NQ - 1)
    mc[0] = weight_gradient((1 - core) * hw).astype(bf16)
    mc_first = send(mc.at[0], mc_in.at[0], mc_s.at[0], mc_r.at[0], sibling)
    for q in range(1, NQ):
        mc[q] = weight_gradient((1 - core) * hw + q * qw).astype(bf16)
    mc_rest = send(mc.at[rest], mc_in.at[rest], mc_s.at[1], mc_r.at[1], sibling)
    for q in range(NQ):
        weight_gradient(core * hw + q * qw)

    def chip_sum(q):
        for k in range(NX):
            here = pl.ds(pl.multiple_of(core * hw + q * qw + k * pw, pw), pw)
            mx[k, q] = (m_v[:, here] + mc_in[q, :, k * pw : (k + 1) * pw].astype(f32)).astype(bf16)

    grad = dot(cbuf[...].reshape(TOK, D), wd_v[...], NT)
    mc_first.wait_recv()
    chip_sum(0)
    mx_first, mx_rest = [], []
    for d in x_far:
        other = lax.rem(x + d, NX)
        mx_first.append(send(mx.at[other, 0], mx_in.at[x, 0], mx_s.at[0, d], mx_r.at[0, d], in_x(d)))
    a, u = gate_v[...].astype(f32), up_v[...].astype(f32)
    s = jax.nn.sigmoid(a)
    dg[...] = (grad * u * s * (1.0 + a * (1.0 - s))).astype(bf16)
    du[...] = (grad * (a * s)).astype(bf16)

    def part_tile(j):
        here = pl.ds(j * width, width)
        value = dot(dg[...], wg_v[here, :], NT) + dot(du[...], wu_v[here, :], NT)
        part[:, :, here] = value.astype(bf16).reshape(NY, rows, width)

    tiles = D // width
    for j in range(tiles // 2):
        part_tile(j)

    def give(k, src, to):
        return send(src, ig_in.at[k], ig_s.at[k], ig_r.at[k], to)

    def total_of(ref, count):
        total = ref[0].astype(f32)
        for k in range(1, count):
            total = total + ref[k].astype(f32)
        return total

    for copy in p1_copies:
        copy.wait_recv()
    p2_in[g] = total_of(p1_in, NZ)
    p2_copies = [send(p2_in.at[g], p2_in.at[g], p2_s.at[d], p2_r.at[d], in_group(d)) for d in g_far]

    mc_rest.wait_recv()
    for q in range(1, NQ):
        chip_sum(q)
    for j in range(tiles // 2, tiles):
        part_tile(j)
    ig0 = give(0, part.at[y_opp, A], right)
    ig3 = give(3, part.at[y_opp, B], left)
    ig1 = give(1, part.at[y_right, B], right)
    ig4 = give(4, part.at[y_left, A], left)
    for copy in p2_copies:
        copy.wait_recv()
    t_v[z] = total_of(p2_in, G)
    p3_copies = [send(t_v.at[z], t_v.at[z], p3_s.at[d], p3_r.at[d], in_z(d)) for d in z_far]
    for d in x_far:
        other = lax.rem(x + d, NX)
        src, dst = mx.at[other, rest], mx_in.at[x, rest]
        mx_rest.append(send(src, dst, mx_s.at[1, d], mx_r.at[1, d], in_x(d)))
    mx_in[x] = mx[x]
    for copy in p3_copies:
        copy.wait_recv()

    row_ids = lax.broadcasted_iota(jnp.int32, (RANK, 1), 0)
    tt[...] = t_v[...].reshape(RANK, F) * mean

    def column(k, carry):
        vector = tt[pl.ds(k, 1), :]
        tile = tt[...]
        squares = jnp.sum(vector * vector, axis=1, keepdims=True) + epsilon
        factors = jnp.sum(tile * vector, axis=1, keepdims=True) * (1.0 / squares)
        tt[...] = tile - jnp.where(row_ids > k, factors, 0.0) * vector
        tt[pl.ds(k, 1), :] = vector * lax.rsqrt(squares)
        return carry

    lax.fori_loop(0, RANK, column, 0)
    ts[...] = split(tt[...])

    for copy in mx_first + mx_rest:
        copy.wait_recv()
    m_sum = total_of(mx_in, NX)
    m_sum = jnp.concatenate([m_sum[q] for q in range(NQ)], axis=1)
    m_high = m_sum.astype(bf16)
    m_low = (m_sum - m_high.astype(f32)).astype(bf16)
    r_all = fold(dot(ts[...], m_high)) + dot(ts[:RANK], m_low)
    for k in range(NZ):
        q, h = k % 4, k // 4
        r2[k] = r_all[16 * q : 16 * q + 16, h * zw : (h + 1) * zw].astype(bf16)
    r2_copies = []
    for d in z_far:
        other = lax.rem(z + d, NZ)
        r2_copies.append(send(r2.at[other], r2_in.at[z], r2_s.at[d], r2_r.at[d], in_z(d)))
    r2_in[z] = r2[z]

    def all_left():
        for copy in sent:
            copy.wait_send()
        sent.clear()

    all_left()

    ig0.wait_recv()
    ig_sum[0] = (ig_in[0].astype(f32) + part[y_right, A].astype(f32)).astype(bf16)
    ig2 = give(2, ig_sum.at[0], right)
    ig3.wait_recv()
    ig_sum[1] = (ig_in[3].astype(f32) + part[y_left, B].astype(f32)).astype(bf16)
    ig5 = give(5, ig_sum.at[1], left)

    for copy in r2_copies:
        copy.wait_recv()
    rfull[core, x, z] = (total_of(r2_in, NZ) * mean).astype(bf16)
    own = rfull.at[core, x, z]
    r3_copies = {d: send(own, own, r3_s.at[d], r3_r.at[d], in_z(d)) for d in z_far}

    r4_copies = {}

    def along_x(k):
        piece = rfull.at[core, x, lax.rem(z + NZ - k, NZ)]
        for d in x_far:
            r4_copies[d, k] = send(piece, piece, r4_s.at[d, k], r4_r.at[d, k], in_x(d))

    along_x(0)
    for k in reversed(z_far):
        r3_copies[k].wait_recv()
        along_x(k)
    own = rfull.at[core, x]
    r5_copies = [send(own, own, r5_s.at[0], r5_r.at[0], sibling)]

    ig1.wait_recv()
    ig4.wait_recv()
    ig2.wait_recv()
    own_a = part[y, A].astype(f32) + ig_in[2].astype(f32) + ig_in[4].astype(f32)
    ig_v[A] = own_a.astype(bf16)
    ig5.wait_recv()
    own_b = part[y, B].astype(f32) + ig_in[1].astype(f32) + ig_in[5].astype(f32)
    ig_v[B] = own_b.astype(bf16)

    for d in reversed(x_far):
        for k in range(NZ):
            r4_copies[d, k].wait_recv()
        came = rfull.at[core, lax.rem(x + NX - d, NX)]
        r5_copies.append(send(came, came, r5_s.at[d], r5_r.at[d], sibling))
    for copy in r5_copies:
        copy.wait_recv()
    all_left()


def finish(ig_v, tt, rfull, m_v, ig, left_out, right_out, err, right_v, err_v, sems):
    RANK, F = tt.shape
    D = m_v.shape[1]
    hw = D // NC
    qw = hw // NQ
    pw = qw // NX
    zw = NQ * pw // (NZ // 4)
    copies = [
        pltpu.make_async_copy(ig_v, ig, sems.at[0]),
        pltpu.make_async_copy(tt, left_out, sems.at[1]),
    ]
    for copy in copies:
        copy.start()
    high = tt[...].astype(bf16).astype(f32)
    both = jnp.concatenate([high, tt[...] - high], axis=0).T.astype(bf16)
    for k in range(NC * NQ):
        h, at = divmod(k % NQ * pw, zw)
        blocks = []
        for chip in range(NX):
            rows = [rfull[k // NQ, chip, 4 * h + q, :, at : at + pw] for q in range(4)]
            blocks.append(jnp.concatenate(rows, axis=0))
        block = jnp.concatenate(blocks, axis=1)
        here = pl.ds(k * qw, qw)
        right_v[:, here] = block.astype(f32)
        update = dot(both, jnp.concatenate([block, block], axis=0))
        err_v[:, here] = (m_v[:, here] - update).astype(bf16)
        copies.append(pltpu.make_async_copy(err_v.at[:, here], err.at[:, here], sems.at[3 + k]))
        copies[-1].start()
    copies.append(pltpu.make_async_copy(right_v, right_out, sems.at[2]))
    copies[-1].start()
    for copy in copies:
        copy.wait()


def shards(cotangent, gate_pre, up_pre, down_weight, gate_weight, up_weight, error_in, factor_in):
    G = NX * NC
    rows, D = cotangent.shape
    half = rows // 2
    TOK = NY * rows
    F = down_weight.shape[0]
    RANK = factor_in.shape[1]
    hw = D // NC
    qw = hw // NQ
    pw = qw // NX
    zw = NQ * pw // (NZ // 4)
    VM = pltpu.VMEM
    DMA = pltpu.SemaphoreType.DMA
    piece = RANK // NZ
    scratch = [
        VM((NY, rows, D), bf16), VM((F, D), bf16), VM((D, F), bf16), VM((D, F), bf16),
        VM((F, D), bf16), VM((RANK, D), f32), VM((2 * RANK, D), bf16),
        VM((TOK, F), bf16), VM((TOK, F), bf16), VM((TOK, F), bf16), VM((F, TOK), bf16),
        VM((NY, rows, RANK), f32), VM((RANK, F), f32), VM((TOK, F), bf16), VM((TOK, F), bf16),
        VM((NY, rows, D), bf16), VM((6, half, D), bf16), VM((2, half, D), bf16),
        VM((NZ, piece, F), f32), VM((NZ, piece, F), f32), VM((G, piece, F), f32), VM((NZ, piece, F), f32),
        VM((2 * RANK, F), bf16), VM((NQ, F, qw), bf16), VM((NQ, F, qw), bf16),
        VM((NX, NQ, F, pw), bf16), VM((NX, NQ, F, pw), bf16), VM((NZ, 16, zw), bf16), VM((NZ, 16, zw), bf16),
        DMA((8,)), DMA((6,)), DMA((6,)),
        DMA((NZ,)), DMA((NZ,)), DMA((G,)), DMA((G,)), DMA((NZ,)), DMA((NZ,)),
        DMA((2,)), DMA((2,)), DMA((2, NX)), DMA((2, NX)), DMA((NZ,)), DMA((NZ,)), DMA((NZ,)), DMA((NZ,)),
        DMA((NX, NZ)), DMA((NX, NZ)), DMA((NX,)), DMA((NX,)), DMA((6,)), DMA((6,)),
    ]
    in_vmem = pl.BlockSpec(memory_space=pltpu.VMEM)
    anywhere = pl.BlockSpec(memory_space=pl.ANY)
    held = pl.pallas_call(
        kernel,
        out_shape=(VM((rows, D), bf16), VM((RANK, F), f32), VM((NC, NX, NZ, 16, zw), bf16), VM((F, D), f32)),
        in_specs=[anywhere] * 8,
        out_specs=(in_vmem,) * 4,
        scratch_shapes=scratch,
        compiler_params=pltpu.CompilerParams(
            collective_id=0, has_side_effects=True, vmem_limit_bytes=VMEM_MIB * 1024 * 1024
        ),
        cost_estimate=pl.CostEstimate(flops=4 * 10**9, bytes_accessed=17 * 10**6, transcendentals=10**5),
    )(cotangent, gate_pre, up_pre, down_weight, gate_weight, up_weight, error_in[0], factor_in[0])
    shape = jax.ShapeDtypeStruct
    input_grad, left_t, right, error_out = pl.pallas_call(
        finish,
        out_shape=(shape((rows, D), bf16), shape((RANK, F), f32), shape((RANK, D), f32), shape((F, D), bf16)),
        in_specs=[in_vmem] * 4,
        out_specs=(anywhere,) * 4,
        scratch_shapes=[VM((RANK, D), f32), VM((F, D), bf16), DMA((3 + NC * NQ,))],
        compiler_params=pltpu.CompilerParams(vmem_limit_bytes=16 * 1024 * 1024),
        cost_estimate=pl.CostEstimate(flops=3 * 10**8, bytes_accessed=9 * 10**6, transcendentals=0),
    )(*held)
    return (input_grad, left_t.T, right[None], error_out[None])


def solution(mesh):
    in_specs = (
        P(("dp", "tensor"), None),
        P("dp", "tensor"),
        P("dp", "tensor"),
        P("tensor", None),
        P(None, "tensor"),
        P(None, "tensor"),
        P("dp", "tensor", None),
        P("tensor", None, None),
    )
    out_specs = (
        P(("dp", "tensor"), None),
        P("tensor", None),
        P("tensor", None, None),
        P("dp", "tensor", None),
    )
    return jax.shard_map(shards, mesh=mesh, in_specs=in_specs, out_specs=out_specs, check_vma=False)
```

```python
import functools

import jax
import jax.numpy as jnp
from jax import lax
from jax.experimental import pallas as pl
from jax.experimental.pallas import tpu as pltpu
from jax.sharding import PartitionSpec as P

epsilon = 1e-06
NX, NZ, NC = 4, 8, 2
NY = 4
VMEM_MIB = 57
NQ = 4
MESH = pl.DeviceIdType.MESH
f32, bf16 = jnp.float32, jnp.bfloat16
NN = (((1,), (0,)), ((), ()))
NT = (((1,), (1,)), ((), ()))


def dot(a, b, dims=NN):
    return lax.dot_general(a, b, dims, preferred_element_type=f32)


def split(a):
    high = a.astype(bf16)
    low = (a - high.astype(f32)).astype(bf16)
    return jnp.concatenate([high, low], axis=0)


def fold(a):
    half = a.shape[0] // 2
    return a[:half] + a[half:]


def kernel(
    c, gate, up, wd, wg, wu, e, f,
    ig_v, tt, rfull, m_v,
    cbuf, wd_v, wg_v, wu_v, e_v, f_v, fs, gate_v, up_v, hid, hid_t, pe, dg, du,
    part, ig_in, ig_sum,
    p1, p1_in, p2_in, t_v, ts, mc, mc_in, mx, mx_in, r2, r2_in,
    load, ag_s, ag_r, p1_s, p1_r, p2_s, p2_r, p3_s, p3_r,
    mc_s, mc_r, mx_s, mx_r, r2_s, r2_r, r3_s, r3_r, r4_s, r4_r, r5_s, r5_r, ig_s, ig_r,
):
    G = NX * NC
    rows, D = c.shape
    half = rows // 2
    TOK = NY * rows
    F = wd.shape[0]
    RANK = f.shape[0]
    hw = D // NC
    qw = hw // NQ
    pw = qw // NX
    zw = NQ * pw // (NZ // 4)
    width = min(1024, hw)
    mean = 1.0 / (NX * NZ * NC)

    dp, y = lax.axis_index("dp"), lax.axis_index("tensor")
    core = lax.rem(dp, NC)
    z = lax.rem(dp // NC, NZ)
    x = dp // (NC * NZ)
    g = x * NC + core
    y_right, y_left, y_opp = (lax.rem(y + k, NY) for k in (1, 3, 2))

    def in_group(d):
        other = lax.rem(g + d, G)
        return (((other // NC) * NZ + z) * NC + lax.rem(other, NC), y)

    def in_x(d):
        return ((lax.rem(x + d, NX) * NZ + z) * NC + core, y)

    def in_z(d):
        return ((x * NZ + lax.rem(z + d, NZ)) * NC + core, y)

    sibling = (dp + 1 - 2 * core, y)

    z_far = sorted(range(1, NZ), key=lambda d: -min(d, NZ - d))
    x_far = sorted(range(1, NX), key=lambda d: -min(d, NX - d))
    g_far = sorted(range(1, G), key=lambda d: -min(d // NC, NX - d // NC))

    mine = cbuf.at[y]
    pairs = [(c, mine), (f, f_v), (e, e_v), (gate, gate_v), (up, up_v), (wd, wd_v), (wg, wg_v), (wu, wu_v)]
    loads = [pltpu.make_async_copy(a, b, load.at[k]) for k, (a, b) in enumerate(pairs)]
    for copy in loads:
        copy.start()

    barrier = pltpu.get_barrier_semaphore()
    partners = [(dp, y_right), (dp, y_left)]
    partners += [in_group(d) for d in range(1, G)] + [in_z(d) for d in range(1, NZ)]
    for other in partners:
        pl.semaphore_signal(barrier, inc=1, device_id=other, device_id_type=MESH)
    pl.semaphore_wait(barrier, len(partners))

    sent = []

    def send(src, dst, s, r, to):
        copy = pltpu.make_async_remote_copy(
            src_ref=src, dst_ref=dst, send_sem=s, recv_sem=r, device_id=to, device_id_type=MESH
        )
        copy.start()
        sent.append(copy)
        return copy

    right, left = (dp, y_right), (dp, y_left)
    A, B = pl.ds(0, half), pl.ds(half, half)

    def gather(k, src, dst, to):
        return send(src, dst, ag_s.at[k], ag_r.at[k], to)

    from_left_a = gather(0, c.at[A], cbuf.at[y, A], right)
    from_right_b = gather(1, c.at[B], cbuf.at[y, B], left)

    loads[1].wait()
    fs[...] = split(f_v[...])
    loads[2].wait()
    pe[...] = fold(dot(fs[...], e_v[...], NT))
    loads[3].wait()
    loads[4].wait()
    a, u = gate_v[...].astype(f32), up_v[...].astype(f32)
    hidden = a * jax.nn.sigmoid(a) * u
    hidden = hidden.astype(bf16).astype(f32)
    hid[...] = hidden.astype(bf16)
    hid_t[...] = hidden.T.astype(bf16)

    from_left_b = gather(2, c.at[B], cbuf.at[y, B], right)
    from_right_a = gather(3, c.at[A], cbuf.at[y, A], left)

    def left_of_block(slot):
        block = fold(dot(fs[...], cbuf[slot], NT))
        return fold(dot(split(block), hid[pl.ds(pl.multiple_of(slot * rows, rows), rows), :]))

    loads[0].wait()
    pe[...] += left_of_block(y)

    from_left_a.wait_recv()
    from_opp_a = gather(4, cbuf.at[y_left, A], cbuf.at[y_left, A], right)
    from_right_b.wait_recv()
    from_opp_b = gather(5, cbuf.at[y_right, B], cbuf.at[y_right, B], left)
    from_left_b.wait_recv()
    pe[...] += left_of_block(y_left)
    from_right_a.wait_recv()
    pe[...] += left_of_block(y_right)
    for k in (5, 6, 7):
        loads[k].wait()
    from_opp_a.wait_recv()
    from_opp_b.wait_recv()
    p_all = left_of_block(y_opp) + pe[...]

    p1[...] = p_all.reshape(NZ, RANK // NZ, F)
    p1_copies = []
    for d in z_far:
        other = lax.rem(z + d, NZ)
        p1_copies.append(send(p1.at[other], p1_in.at[z], p1_s.at[d], p1_r.at[d], in_z(d)))
    p1_in[z] = p1[z]

    def weight_gradient(first):
        here = pl.ds(pl.multiple_of(first, qw), qw)
        block = cbuf[:, :, here].reshape(TOK, qw)
        value = dot(hid_t[...], block) + e_v[:, here].astype(f32)
        m_v[:, here] = value
        return value

    rest = pl.ds(1, NQ - 1)
    mc[0] = weight_gradient((1 - core) * hw).astype(bf16)
    mc_first = send(mc.at[0], mc_in.at[0], mc_s.at[0], mc_r.at[0], sibling)
    weight_gradient(core * hw)
    for q in range(1, NQ):
        mc[q] = weight_gradient((1 - core) * hw + q * qw).astype(bf16)
    mc_rest = send(mc.at[rest], mc_in.at[rest], mc_s.at[1], mc_r.at[1], sibling)

    def chip_sum(q):
        for k in range(NX):
            here = pl.ds(pl.multiple_of(core * hw + q * qw + k * pw, pw), pw)
            mx[k, q] = (m_v[:, here] + mc_in[q, :, k * pw : (k + 1) * pw].astype(f32)).astype(bf16)

    mc_first.wait_recv()
    chip_sum(0)
    mx_first, mx_rest = [], []
    for d in x_far:
        other = lax.rem(x + d, NX)
        mx_first.append(send(mx.at[other, 0], mx_in.at[x, 0], mx_s.at[0, d], mx_r.at[0, d], in_x(d)))

    def total_of(ref, count):
        total = ref[0].astype(f32)
        for k in range(1, count):
            total = total + ref[k].astype(f32)
        return total

    for copy in p1_copies:
        copy.wait_recv()
    p2_in[g] = total_of(p1_in, NZ)
    p2_copies = [send(p2_in.at[g], p2_in.at[g], p2_s.at[d], p2_r.at[d], in_group(d)) for d in g_far]

    for q in range(1, NQ):
        weight_gradient(core * hw + q * qw)
    mc_rest.wait_recv()
    for q in range(1, NQ):
        chip_sum(q)

    grad = dot(cbuf[...].reshape(TOK, D), wd_v[...], NT)
    a, u = gate_v[...].astype(f32), up_v[...].astype(f32)
    s = jax.nn.sigmoid(a)
    dg[...] = (grad * u * s * (1.0 + a * (1.0 - s))).astype(bf16)
    du[...] = (grad * (a * s)).astype(bf16)

    for copy in p2_copies:
        copy.wait_recv()
    t_v[z] = total_of(p2_in, G)
    p3_copies = [send(t_v.at[z], t_v.at[z], p3_s.at[d], p3_r.at[d], in_z(d)) for d in z_far]
    for d in x_far:
        other = lax.rem(x + d, NX)
        src, dst = mx.at[other, rest], mx_in.at[x, rest]
        mx_rest.append(send(src, dst, mx_s.at[1, d], mx_r.at[1, d], in_x(d)))
    mx_in[x] = mx[x]

    def part_tile(j):
        here = pl.ds(j * width, width)
        value = dot(dg[...], wg_v[here, :], NT) + dot(du[...], wu_v[here, :], NT)
        part[:, :, here] = value.astype(bf16).reshape(NY, rows, width)

    for j in range(D // width):
        part_tile(j)

    def give(k, src, to):
        return send(src, ig_in.at[k], ig_s.at[k], ig_r.at[k], to)

    ig0 = give(0, part.at[y_opp, A], right)
    ig3 = give(3, part.at[y_opp, B], left)
    ig1 = give(1, part.at[y_right, B], right)
    ig4 = give(4, part.at[y_left, A], left)
    for copy in p3_copies:
        copy.wait_recv()

    row_ids = lax.broadcasted_iota(jnp.int32, (RANK, 1), 0)
    tt[...] = t_v[...].reshape(RANK, F) * mean

    def column(k, carry):
        vector = tt[pl.ds(k, 1), :]
        tile = tt[...]
        squares = jnp.sum(vector * vector, axis=1, keepdims=True) + epsilon
        factors = jnp.sum(tile * vector, axis=1, keepdims=True) * (1.0 / squares)
        tt[...] = tile - jnp.where(row_ids > k, factors, 0.0) * vector
        tt[pl.ds(k, 1), :] = vector * lax.rsqrt(squares)
        return carry

    lax.fori_loop(0, RANK, column, 0)
    ts[...] = split(tt[...])

    for copy in mx_first + mx_rest:
        copy.wait_recv()
    m_sum = total_of(mx_in, NX)
    m_sum = jnp.concatenate([m_sum[q] for q in range(NQ)], axis=1)
    m_high = m_sum.astype(bf16)
    m_low = (m_sum - m_high.astype(f32)).astype(bf16)
    r_all = fold(dot(ts[...], m_high)) + dot(ts[:RANK], m_low)
    for k in range(NZ):
        q, h = k % 4, k // 4
        r2[k] = r_all[16 * q : 16 * q + 16, h * zw : (h + 1) * zw].astype(bf16)
    r2_copies = []
    for d in z_far:
        other = lax.rem(z + d, NZ)
        r2_copies.append(send(r2.at[other], r2_in.at[z], r2_s.at[d], r2_r.at[d], in_z(d)))
    r2_in[z] = r2[z]

    def all_left():
        for copy in sent:
            copy.wait_send()
        sent.clear()

    all_left()

    ig0.wait_recv()
    ig_sum[0] = (ig_in[0].astype(f32) + part[y_right, A].astype(f32)).astype(bf16)
    ig2 = give(2, ig_sum.at[0], right)
    ig3.wait_recv()
    ig_sum[1] = (ig_in[3].astype(f32) + part[y_left, B].astype(f32)).astype(bf16)
    ig5 = give(5, ig_sum.at[1], left)

    for copy in r2_copies:
        copy.wait_recv()
    rfull[core, x, z] = (total_of(r2_in, NZ) * mean).astype(bf16)
    own = rfull.at[core, x, z]
    r3_copies = {d: send(own, own, r3_s.at[d], r3_r.at[d], in_z(d)) for d in z_far}

    r4_copies = {}

    def along_x(k):
        piece = rfull.at[core, x, lax.rem(z + NZ - k, NZ)]
        for d in x_far:
            r4_copies[d, k] = send(piece, piece, r4_s.at[d, k], r4_r.at[d, k], in_x(d))

    along_x(0)
    for k in reversed(z_far):
        r3_copies[k].wait_recv()
        along_x(k)
    own = rfull.at[core, x]
    r5_copies = [send(own, own, r5_s.at[0], r5_r.at[0], sibling)]

    ig1.wait_recv()
    ig4.wait_recv()
    ig2.wait_recv()
    own_a = part[y, A].astype(f32) + ig_in[2].astype(f32) + ig_in[4].astype(f32)
    ig_v[A] = own_a.astype(bf16)
    ig5.wait_recv()
    own_b = part[y, B].astype(f32) + ig_in[1].astype(f32) + ig_in[5].astype(f32)
    ig_v[B] = own_b.astype(bf16)

    for d in reversed(x_far):
        for k in range(NZ):
            r4_copies[d, k].wait_recv()
        came = rfull.at[core, lax.rem(x + NX - d, NX)]
        r5_copies.append(send(came, came, r5_s.at[d], r5_r.at[d], sibling))
    for copy in r5_copies:
        copy.wait_recv()
    all_left()


def finish(ig_v, tt, rfull, m_v, ig, left_out, right_out, err, right_v, err_v, sems):
    RANK, F = tt.shape
    D = m_v.shape[1]
    hw = D // NC
    qw = hw // NQ
    pw = qw // NX
    zw = NQ * pw // (NZ // 4)
    copies = [
        pltpu.make_async_copy(ig_v, ig, sems.at[0]),
        pltpu.make_async_copy(tt, left_out, sems.at[1]),
    ]
    for copy in copies:
        copy.start()
    high = tt[...].astype(bf16).astype(f32)
    both = jnp.concatenate([high, tt[...] - high], axis=0).T.astype(bf16)
    for k in range(NC * NQ):
        h, at = divmod(k % NQ * pw, zw)
        blocks = []
        for chip in range(NX):
            rows = [rfull[k // NQ, chip, 4 * h + q, :, at : at + pw] for q in range(4)]
            blocks.append(jnp.concatenate(rows, axis=0))
        block = jnp.concatenate(blocks, axis=1)
        here = pl.ds(k * qw, qw)
        right_v[:, here] = block.astype(f32)
        update = dot(both, jnp.concatenate([block, block], axis=0))
        err_v[:, here] = (m_v[:, here] - update).astype(bf16)
        copies.append(pltpu.make_async_copy(err_v.at[:, here], err.at[:, here], sems.at[2 + 2 * k]))
        copies[-1].start()
        copies.append(pltpu.make_async_copy(right_v.at[:, here], right_out.at[:, here], sems.at[3 + 2 * k]))
        copies[-1].start()
    for copy in copies:
        copy.wait()


def shards(cotangent, gate_pre, up_pre, down_weight, gate_weight, up_weight, error_in, factor_in):
    G = NX * NC
    rows, D = cotangent.shape
    half = rows // 2
    TOK = NY * rows
    F = down_weight.shape[0]
    RANK = factor_in.shape[1]
    hw = D // NC
    qw = hw // NQ
    pw = qw // NX
    zw = NQ * pw // (NZ // 4)
    VM = pltpu.VMEM
    DMA = pltpu.SemaphoreType.DMA
    piece = RANK // NZ
    scratch = [
        VM((NY, rows, D), bf16), VM((F, D), bf16), VM((D, F), bf16), VM((D, F), bf16),
        VM((F, D), bf16), VM((RANK, D), f32), VM((2 * RANK, D), bf16),
        VM((TOK, F), bf16), VM((TOK, F), bf16), VM((TOK, F), bf16), VM((F, TOK), bf16),
        VM((RANK, F), f32), VM((TOK, F), bf16), VM((TOK, F), bf16),
        VM((NY, rows, D), bf16), VM((6, half, D), bf16), VM((2, half, D), bf16),
        VM((NZ, piece, F), f32), VM((NZ, piece, F), f32), VM((G, piece, F), f32), VM((NZ, piece, F), f32),
        VM((2 * RANK, F), bf16), VM((NQ, F, qw), bf16), VM((NQ, F, qw), bf16),
        VM((NX, NQ, F, pw), bf16), VM((NX, NQ, F, pw), bf16), VM((NZ, 16, zw), bf16), VM((NZ, 16, zw), bf16),
        DMA((8,)), DMA((6,)), DMA((6,)),
        DMA((NZ,)), DMA((NZ,)), DMA((G,)), DMA((G,)), DMA((NZ,)), DMA((NZ,)),
        DMA((2,)), DMA((2,)), DMA((2, NX)), DMA((2, NX)), DMA((NZ,)), DMA((NZ,)), DMA((NZ,)), DMA((NZ,)),
        DMA((NX, NZ)), DMA((NX, NZ)), DMA((NX,)), DMA((NX,)), DMA((6,)), DMA((6,)),
    ]
    in_vmem = pl.BlockSpec(memory_space=pltpu.VMEM)
    anywhere = pl.BlockSpec(memory_space=pl.ANY)
    held = pl.pallas_call(
        kernel,
        out_shape=(VM((rows, D), bf16), VM((RANK, F), f32), VM((NC, NX, NZ, 16, zw), bf16), VM((F, D), f32)),
        in_specs=[anywhere] * 8,
        out_specs=(in_vmem,) * 4,
        scratch_shapes=scratch,
        compiler_params=pltpu.CompilerParams(
            collective_id=0, has_side_effects=True, vmem_limit_bytes=VMEM_MIB * 1024 * 1024
        ),
        cost_estimate=pl.CostEstimate(flops=4 * 10**9, bytes_accessed=17 * 10**6, transcendentals=10**5),
    )(cotangent, gate_pre, up_pre, down_weight, gate_weight, up_weight, error_in[0], factor_in[0])
    shape = jax.ShapeDtypeStruct
    input_grad, left_t, right, error_out = pl.pallas_call(
        finish,
        out_shape=(shape((rows, D), bf16), shape((RANK, F), f32), shape((RANK, D), f32), shape((F, D), bf16)),
        in_specs=[in_vmem] * 4,
        out_specs=(anywhere,) * 4,
        scratch_shapes=[VM((RANK, D), f32), VM((F, D), bf16), DMA((2 + 2 * NC * NQ,))],
        compiler_params=pltpu.CompilerParams(vmem_limit_bytes=16 * 1024 * 1024),
        cost_estimate=pl.CostEstimate(flops=3 * 10**8, bytes_accessed=9 * 10**6, transcendentals=0),
    )(*held)
    return (input_grad, left_t.T, right[None], error_out[None])


def solution(mesh):
    in_specs = (
        P(("dp", "tensor"), None),
        P("dp", "tensor"),
        P("dp", "tensor"),
        P("tensor", None),
        P(None, "tensor"),
        P(None, "tensor"),
        P("dp", "tensor", None),
        P("tensor", None, None),
    )
    out_specs = (
        P(("dp", "tensor"), None),
        P("tensor", None),
        P("tensor", None, None),
        P("dp", "tensor", None),
    )
    return jax.shard_map(shards, mesh=mesh, in_specs=in_specs, out_specs=out_specs, check_vma=False)
```

```python
import functools

import jax
import jax.numpy as jnp
from jax import lax
from jax.experimental import pallas as pl
from jax.experimental.pallas import tpu as pltpu
from jax.sharding import PartitionSpec as P

epsilon = 1e-06
NX, NZ, NC = 4, 8, 2
NY = 4
VMEM_MIB = 57
NQ = 4
MESH = pl.DeviceIdType.MESH
f32, bf16 = jnp.float32, jnp.bfloat16
NN = (((1,), (0,)), ((), ()))
NT = (((1,), (1,)), ((), ()))


def dot(a, b, dims=NN):
    return lax.dot_general(a, b, dims, preferred_element_type=f32)


def split(a):
    high = a.astype(bf16)
    low = (a - high.astype(f32)).astype(bf16)
    return jnp.concatenate([high, low], axis=0)


def fold(a):
    half = a.shape[0] // 2
    return a[:half] + a[half:]


def kernel(
    c, gate, up, wd, wg, wu, e, f,
    ig_v, tt, rfull, m_v,
    cbuf, wd_v, wg_v, wu_v, e_v, f_v, fs, gate_v, up_v, hid, hid_t, pe, dg, du,
    part, ig_in, ig_sum,
    p1, p1_in, p2_in, t_v, ts, mc, mc_in, mx, mx_in, r2, r2_in,
    load, ag_s, ag_r, p1_s, p1_r, p2_s, p2_r, p3_s, p3_r,
    mc_s, mc_r, mx_s, mx_r, r2_s, r2_r, r3_s, r3_r, r4_s, r4_r, r5_s, r5_r, ig_s, ig_r,
):
    G = NX * NC
    rows, D = c.shape
    half = rows // 2
    TOK = NY * rows
    F = wd.shape[0]
    RANK = f.shape[0]
    hw = D // NC
    qw = hw // NQ
    pw = qw // NX
    zw = NQ * pw // (NZ // 4)
    width = min(1024, hw)
    mean = 1.0 / (NX * NZ * NC)

    dp, y = lax.axis_index("dp"), lax.axis_index("tensor")
    core = lax.rem(dp, NC)
    z = lax.rem(dp // NC, NZ)
    x = dp // (NC * NZ)
    g = x * NC + core
    y_right, y_left, y_opp = (lax.rem(y + k, NY) for k in (1, 3, 2))

    def in_group(d):
        other = lax.rem(g + d, G)
        return (((other // NC) * NZ + z) * NC + lax.rem(other, NC), y)

    def in_x(d):
        return ((lax.rem(x + d, NX) * NZ + z) * NC + core, y)

    def in_z(d):
        return ((x * NZ + lax.rem(z + d, NZ)) * NC + core, y)

    sibling = (dp + 1 - 2 * core, y)

    z_far = sorted(range(1, NZ), key=lambda d: -min(d, NZ - d))
    x_far = sorted(range(1, NX), key=lambda d: -min(d, NX - d))
    g_far = sorted(range(1, G), key=lambda d: -min(d // NC, NX - d // NC))

    mine = cbuf.at[y]
    pairs = [(c, mine), (f, f_v), (e, e_v), (gate, gate_v), (up, up_v), (wd, wd_v), (wg, wg_v), (wu, wu_v)]

    barrier = pltpu.get_barrier_semaphore()
    partners = [in_z(d) for d in z_far] + [in_group(d) for d in g_far] + [(dp, y_right), (dp, y_left)]
    for other in partners:
        pl.semaphore_signal(barrier, inc=1, device_id=other, device_id_type=MESH)
    loads = [pltpu.make_async_copy(a, b, load.at[k]) for k, (a, b) in enumerate(pairs)]
    for copy in loads:
        copy.start()
    pl.semaphore_wait(barrier, len(partners))

    sent = []

    def send(src, dst, s, r, to):
        copy = pltpu.make_async_remote_copy(
            src_ref=src, dst_ref=dst, send_sem=s, recv_sem=r, device_id=to, device_id_type=MESH
        )
        copy.start()
        sent.append(copy)
        return copy

    right, left = (dp, y_right), (dp, y_left)
    A, B = pl.ds(0, half), pl.ds(half, half)

    def gather(k, src, dst, to):
        return send(src, dst, ag_s.at[k], ag_r.at[k], to)

    from_left_a = gather(0, c.at[A], cbuf.at[y, A], right)
    from_right_b = gather(1, c.at[B], cbuf.at[y, B], left)

    loads[1].wait()
    fs[...] = split(f_v[...])
    loads[2].wait()
    pe[...] = fold(dot(fs[...], e_v[...], NT))
    loads[3].wait()
    loads[4].wait()
    a, u = gate_v[...].astype(f32), up_v[...].astype(f32)
    hidden = a * jax.nn.sigmoid(a) * u
    hidden = hidden.astype(bf16).astype(f32)
    hid[...] = hidden.astype(bf16)
    hid_t[...] = hidden.T.astype(bf16)

    from_left_b = gather(2, c.at[B], cbuf.at[y, B], right)
    from_right_a = gather(3, c.at[A], cbuf.at[y, A], left)

    def left_of_block(slot):
        block = fold(dot(fs[...], cbuf[slot], NT))
        return fold(dot(split(block), hid[pl.ds(pl.multiple_of(slot * rows, rows), rows), :]))

    loads[0].wait()
    pe[...] += left_of_block(y)

    from_left_a.wait_recv()
    from_opp_a = gather(4, cbuf.at[y_left, A], cbuf.at[y_left, A], right)
    from_right_b.wait_recv()
    from_opp_b = gather(5, cbuf.at[y_right, B], cbuf.at[y_right, B], left)
    from_left_b.wait_recv()
    pe[...] += left_of_block(y_left)
    from_right_a.wait_recv()
    pe[...] += left_of_block(y_right)
    for k in (5, 6, 7):
        loads[k].wait()
    from_opp_a.wait_recv()
    from_opp_b.wait_recv()
    p_all = left_of_block(y_opp) + pe[...]

    p1[...] = p_all.reshape(NZ, RANK // NZ, F)
    p1_copies = []
    for d in z_far:
        other = lax.rem(z + d, NZ)
        p1_copies.append(send(p1.at[other], p1_in.at[z], p1_s.at[d], p1_r.at[d], in_z(d)))
    p1_in[z] = p1[z]

    def weight_gradient(first):
        here = pl.ds(pl.multiple_of(first, qw), qw)
        block = cbuf[:, :, here].reshape(TOK, qw)
        value = dot(hid_t[...], block) + e_v[:, here].astype(f32)
        m_v[:, here] = value
        return value

    rest = pl.ds(1, NQ - 1)
    mc[0] = weight_gradient((1 - core) * hw).astype(bf16)
    mc_first = send(mc.at[0], mc_in.at[0], mc_s.at[0], mc_r.at[0], sibling)
    weight_gradient(core * hw)
    for q in range(1, NQ):
        mc[q] = weight_gradient((1 - core) * hw + q * qw).astype(bf16)
    mc_rest = send(mc.at[rest], mc_in.at[rest], mc_s.at[1], mc_r.at[1], sibling)

    def chip_sum(q):
        for k in range(NX):
            here = pl.ds(pl.multiple_of(core * hw + q * qw + k * pw, pw), pw)
            mx[k, q] = (m_v[:, here] + mc_in[q, :, k * pw : (k + 1) * pw].astype(f32)).astype(bf16)

    mc_first.wait_recv()
    chip_sum(0)
    mx_first, mx_rest = [], []
    for d in x_far:
        other = lax.rem(x + d, NX)
        mx_first.append(send(mx.at[other, 0], mx_in.at[x, 0], mx_s.at[0, d], mx_r.at[0, d], in_x(d)))

    def total_of(ref, count):
        total = ref[0].astype(f32)
        for k in range(1, count):
            total = total + ref[k].astype(f32)
        return total

    for copy in p1_copies:
        copy.wait_recv()
    p2_in[g] = total_of(p1_in, NZ)
    p2_copies = [send(p2_in.at[g], p2_in.at[g], p2_s.at[d], p2_r.at[d], in_group(d)) for d in g_far]

    for q in range(1, NQ):
        weight_gradient(core * hw + q * qw)
    mc_rest.wait_recv()
    for q in range(1, NQ):
        chip_sum(q)

    grad = dot(cbuf[...].reshape(TOK, D), wd_v[...], NT)
    a, u = gate_v[...].astype(f32), up_v[...].astype(f32)
    s = jax.nn.sigmoid(a)
    dg[...] = (grad * u * s * (1.0 + a * (1.0 - s))).astype(bf16)
    du[...] = (grad * (a * s)).astype(bf16)

    for copy in p2_copies:
        copy.wait_recv()
    t_v[z] = total_of(p2_in, G)
    p3_copies = [send(t_v.at[z], t_v.at[z], p3_s.at[d], p3_r.at[d], in_z(d)) for d in z_far]
    for d in x_far:
        other = lax.rem(x + d, NX)
        src, dst = mx.at[other, rest], mx_in.at[x, rest]
        mx_rest.append(send(src, dst, mx_s.at[1, d], mx_r.at[1, d], in_x(d)))
    mx_in[x] = mx[x]

    def part_tile(j):
        here = pl.ds(j * width, width)
        value = dot(dg[...], wg_v[here, :], NT) + dot(du[...], wu_v[here, :], NT)
        part[:, :, here] = value.astype(bf16).reshape(NY, rows, width)

    for j in range(D // width):
        part_tile(j)

    def give(k, src, to):
        return send(src, ig_in.at[k], ig_s.at[k], ig_r.at[k], to)

    ig0 = give(0, part.at[y_opp, A], right)
    ig3 = give(3, part.at[y_opp, B], left)
    ig1 = give(1, part.at[y_right, B], right)
    ig4 = give(4, part.at[y_left, A], left)
    for copy in p3_copies:
        copy.wait_recv()

    row_ids = lax.broadcasted_iota(jnp.int32, (RANK, 1), 0)
    tt[...] = t_v[...].reshape(RANK, F) * mean

    def column(k, carry):
        vector = tt[pl.ds(k, 1), :]
        tile = tt[...]
        squares = jnp.sum(vector * vector, axis=1, keepdims=True) + epsilon
        factors = jnp.sum(tile * vector, axis=1, keepdims=True) * (1.0 / squares)
        tt[...] = tile - jnp.where(row_ids > k, factors, 0.0) * vector
        tt[pl.ds(k, 1), :] = vector * lax.rsqrt(squares)
        return carry

    lax.fori_loop(0, RANK, column, 0)
    ts[...] = split(tt[...])

    for copy in mx_first + mx_rest:
        copy.wait_recv()
    m_sum = total_of(mx_in, NX)
    m_sum = jnp.concatenate([m_sum[q] for q in range(NQ)], axis=1)
    m_high = m_sum.astype(bf16)
    m_low = (m_sum - m_high.astype(f32)).astype(bf16)
    r_all = fold(dot(ts[...], m_high)) + dot(ts[:RANK], m_low)
    for k in range(NZ):
        q, h = k % 4, k // 4
        r2[k] = r_all[16 * q : 16 * q + 16, h * zw : (h + 1) * zw].astype(bf16)
    r2_copies = []
    for d in z_far:
        other = lax.rem(z + d, NZ)
        r2_copies.append(send(r2.at[other], r2_in.at[z], r2_s.at[d], r2_r.at[d], in_z(d)))
    r2_in[z] = r2[z]

    def all_left():
        for copy in sent:
            copy.wait_send()
        sent.clear()

    all_left()

    ig0.wait_recv()
    ig_sum[0] = (ig_in[0].astype(f32) + part[y_right, A].astype(f32)).astype(bf16)
    ig2 = give(2, ig_sum.at[0], right)
    ig3.wait_recv()
    ig_sum[1] = (ig_in[3].astype(f32) + part[y_left, B].astype(f32)).astype(bf16)
    ig5 = give(5, ig_sum.at[1], left)

    for copy in r2_copies:
        copy.wait_recv()
    rfull[core, x, z] = (total_of(r2_in, NZ) * mean).astype(bf16)
    own = rfull.at[core, x, z]
    r3_copies = {d: send(own, own, r3_s.at[d], r3_r.at[d], in_z(d)) for d in z_far}

    r4_copies = {}

    def along_x(k):
        piece = rfull.at[core, x, lax.rem(z + NZ - k, NZ)]
        for d in x_far:
            r4_copies[d, k] = send(piece, piece, r4_s.at[d, k], r4_r.at[d, k], in_x(d))

    along_x(0)
    for k in reversed(z_far):
        r3_copies[k].wait_recv()
        along_x(k)
    own = rfull.at[core, x]
    r5_copies = [send(own, own, r5_s.at[0], r5_r.at[0], sibling)]

    ig1.wait_recv()
    ig4.wait_recv()
    ig2.wait_recv()
    own_a = part[y, A].astype(f32) + ig_in[2].astype(f32) + ig_in[4].astype(f32)
    ig_v[A] = own_a.astype(bf16)
    ig5.wait_recv()
    own_b = part[y, B].astype(f32) + ig_in[1].astype(f32) + ig_in[5].astype(f32)
    ig_v[B] = own_b.astype(bf16)

    for d in reversed(x_far):
        for k in range(NZ):
            r4_copies[d, k].wait_recv()
        came = rfull.at[core, lax.rem(x + NX - d, NX)]
        r5_copies.append(send(came, came, r5_s.at[d], r5_r.at[d], sibling))
    for copy in r5_copies:
        copy.wait_recv()
    all_left()


def finish(ig_v, tt, rfull, m_v, ig, left_out, right_out, err, right_v, err_v, sems):
    RANK, F = tt.shape
    D = m_v.shape[1]
    hw = D // NC
    qw = hw // NQ
    pw = qw // NX
    zw = NQ * pw // (NZ // 4)
    copies = [
        pltpu.make_async_copy(ig_v, ig, sems.at[0]),
        pltpu.make_async_copy(tt, left_out, sems.at[1]),
    ]
    for copy in copies:
        copy.start()
    high = tt[...].astype(bf16).astype(f32)
    both = jnp.concatenate([high, tt[...] - high], axis=0).T.astype(bf16)
    for k in range(NC * NQ):
        h, at = divmod(k % NQ * pw, zw)
        blocks = []
        for chip in range(NX):
            rows = [rfull[k // NQ, chip, 4 * h + q, :, at : at + pw] for q in range(4)]
            blocks.append(jnp.concatenate(rows, axis=0))
        block = jnp.concatenate(blocks, axis=1)
        here = pl.ds(k * qw, qw)
        right_v[:, here] = block.astype(f32)
        update = dot(both, jnp.concatenate([block, block], axis=0))
        err_v[:, here] = (m_v[:, here] - update).astype(bf16)
        copies.append(pltpu.make_async_copy(err_v.at[:, here], err.at[:, here], sems.at[2 + 2 * k]))
        copies[-1].start()
        copies.append(pltpu.make_async_copy(right_v.at[:, here], right_out.at[:, here], sems.at[3 + 2 * k]))
        copies[-1].start()
    for copy in copies:
        copy.wait()


def shards(cotangent, gate_pre, up_pre, down_weight, gate_weight, up_weight, error_in, factor_in):
    G = NX * NC
    rows, D = cotangent.shape
    half = rows // 2
    TOK = NY * rows
    F = down_weight.shape[0]
    RANK = factor_in.shape[1]
    hw = D // NC
    qw = hw // NQ
    pw = qw // NX
    zw = NQ * pw // (NZ // 4)
    VM = pltpu.VMEM
    DMA = pltpu.SemaphoreType.DMA
    piece = RANK // NZ
    scratch = [
        VM((NY, rows, D), bf16), VM((F, D), bf16), VM((D, F), bf16), VM((D, F), bf16),
        VM((F, D), bf16), VM((RANK, D), f32), VM((2 * RANK, D), bf16),
        VM((TOK, F), bf16), VM((TOK, F), bf16), VM((TOK, F), bf16), VM((F, TOK), bf16),
        VM((RANK, F), f32), VM((TOK, F), bf16), VM((TOK, F), bf16),
        VM((NY, rows, D), bf16), VM((6, half, D), bf16), VM((2, half, D), bf16),
        VM((NZ, piece, F), f32), VM((NZ, piece, F), f32), VM((G, piece, F), f32), VM((NZ, piece, F), f32),
        VM((2 * RANK, F), bf16), VM((NQ, F, qw), bf16), VM((NQ, F, qw), bf16),
        VM((NX, NQ, F, pw), bf16), VM((NX, NQ, F, pw), bf16), VM((NZ, 16, zw), bf16), VM((NZ, 16, zw), bf16),
        DMA((8,)), DMA((6,)), DMA((6,)),
        DMA((NZ,)), DMA((NZ,)), DMA((G,)), DMA((G,)), DMA((NZ,)), DMA((NZ,)),
        DMA((2,)), DMA((2,)), DMA((2, NX)), DMA((2, NX)), DMA((NZ,)), DMA((NZ,)), DMA((NZ,)), DMA((NZ,)),
        DMA((NX, NZ)), DMA((NX, NZ)), DMA((NX,)), DMA((NX,)), DMA((6,)), DMA((6,)),
    ]
    in_vmem = pl.BlockSpec(memory_space=pltpu.VMEM)
    anywhere = pl.BlockSpec(memory_space=pl.ANY)
    held = pl.pallas_call(
        kernel,
        out_shape=(VM((rows, D), bf16), VM((RANK, F), f32), VM((NC, NX, NZ, 16, zw), bf16), VM((F, D), f32)),
        in_specs=[anywhere] * 8,
        out_specs=(in_vmem,) * 4,
        scratch_shapes=scratch,
        compiler_params=pltpu.CompilerParams(
            collective_id=0, has_side_effects=True, vmem_limit_bytes=VMEM_MIB * 1024 * 1024
        ),
        cost_estimate=pl.CostEstimate(flops=4 * 10**9, bytes_accessed=17 * 10**6, transcendentals=10**5),
    )(cotangent, gate_pre, up_pre, down_weight, gate_weight, up_weight, error_in[0], factor_in[0])
    shape = jax.ShapeDtypeStruct
    input_grad, left_t, right, error_out = pl.pallas_call(
        finish,
        out_shape=(shape((rows, D), bf16), shape((RANK, F), f32), shape((RANK, D), f32), shape((F, D), bf16)),
        in_specs=[in_vmem] * 4,
        out_specs=(anywhere,) * 4,
        scratch_shapes=[VM((RANK, D), f32), VM((F, D), bf16), DMA((2 + 2 * NC * NQ,))],
        compiler_params=pltpu.CompilerParams(vmem_limit_bytes=16 * 1024 * 1024),
        cost_estimate=pl.CostEstimate(flops=3 * 10**8, bytes_accessed=9 * 10**6, transcendentals=0),
    )(*held)
    return (input_grad, left_t.T, right[None], error_out[None])


def solution(mesh):
    in_specs = (
        P(("dp", "tensor"), None),
        P("dp", "tensor"),
        P("dp", "tensor"),
        P("tensor", None),
        P(None, "tensor"),
        P(None, "tensor"),
        P("dp", "tensor", None),
        P("tensor", None, None),
    )
    out_specs = (
        P(("dp", "tensor"), None),
        P("tensor", None),
        P("tensor", None, None),
        P("dp", "tensor", None),
    )
    return jax.shard_map(shards, mesh=mesh, in_specs=in_specs, out_specs=out_specs, check_vma=False)
```

```python
import functools

import jax
import jax.numpy as jnp
from jax import lax
from jax.experimental import pallas as pl
from jax.experimental.pallas import tpu as pltpu
from jax.sharding import PartitionSpec as P

epsilon = 1e-06
NX, NZ, NC = 4, 8, 2
NY = 4
VMEM_MIB = 57
NQ = 4
MESH = pl.DeviceIdType.MESH
f32, bf16 = jnp.float32, jnp.bfloat16
NN = (((1,), (0,)), ((), ()))
NT = (((1,), (1,)), ((), ()))


def dot(a, b, dims=NN):
    return lax.dot_general(a, b, dims, preferred_element_type=f32)


def split(a):
    high = a.astype(bf16)
    low = (a - high.astype(f32)).astype(bf16)
    return jnp.concatenate([high, low], axis=0)


def fold(a):
    half = a.shape[0] // 2
    return a[:half] + a[half:]


def kernel(
    c, gate, up, wd, wg, wu, e, f,
    ig_v, tt, rfull, m_v,
    cbuf, wd_v, wg_v, wu_v, e_v, f_v, fs, gate_v, up_v, hid, hid_t, pe, dg, du,
    part, ig_in, ig_sum,
    p1, p1_in, p2_in, t_v, ts, mc, mc_in, mx, mx_in, r2, r2_in,
    load, ag_s, ag_r, p1_s, p1_r, p2_s, p2_r, p3_s, p3_r,
    mc_s, mc_r, mx_s, mx_r, r2_s, r2_r, r3_s, r3_r, r4_s, r4_r, r5_s, r5_r, ig_s, ig_r,
):
    G = NX * NC
    rows, D = c.shape
    half = rows // 2
    TOK = NY * rows
    F = wd.shape[0]
    RANK = f.shape[0]
    hw = D // NC
    qw = hw // NQ
    pw = qw // NX
    zw = NQ * pw // (NZ // 4)
    width = min(1024, hw)
    mean = 1.0 / (NX * NZ * NC)

    dp, y = lax.axis_index("dp"), lax.axis_index("tensor")
    core = lax.rem(dp, NC)
    z = lax.rem(dp // NC, NZ)
    x = dp // (NC * NZ)
    g = x * NC + core
    y_right, y_left, y_opp = (lax.rem(y + k, NY) for k in (1, 3, 2))

    def in_group(d):
        other = lax.rem(g + d, G)
        return (((other // NC) * NZ + z) * NC + lax.rem(other, NC), y)

    def in_x(d):
        return ((lax.rem(x + d, NX) * NZ + z) * NC + core, y)

    def in_z(d):
        return ((x * NZ + lax.rem(z + d, NZ)) * NC + core, y)

    sibling = (dp + 1 - 2 * core, y)

    z_far = sorted(range(1, NZ), key=lambda d: -min(d, NZ - d))
    x_far = sorted(range(1, NX), key=lambda d: -min(d, NX - d))
    g_far = sorted(range(1, G), key=lambda d: -min(d // NC, NX - d // NC))

    mine = cbuf.at[y]
    pairs = [(c, mine), (f, f_v), (e, e_v), (gate, gate_v), (up, up_v), (wd, wd_v), (wg, wg_v), (wu, wu_v)]

    barrier = pltpu.get_barrier_semaphore()
    partners = [in_z(d) for d in z_far] + [in_group(d) for d in g_far] + [(dp, y_right), (dp, y_left)]
    for other in partners:
        pl.semaphore_signal(barrier, inc=1, device_id=other, device_id_type=MESH)
    loads = [pltpu.make_async_copy(a, b, load.at[k]) for k, (a, b) in enumerate(pairs)]
    for copy in loads:
        copy.start()
    pl.semaphore_wait(barrier, len(partners))

    sent = []

    def send(src, dst, s, r, to):
        copy = pltpu.make_async_remote_copy(
            src_ref=src, dst_ref=dst, send_sem=s, recv_sem=r, device_id=to, device_id_type=MESH
        )
        copy.start()
        sent.append(copy)
        return copy

    right, left = (dp, y_right), (dp, y_left)
    A, B = pl.ds(0, half), pl.ds(half, half)

    def gather(k, src, dst, to):
        return send(src, dst, ag_s.at[k], ag_r.at[k], to)

    from_left_a = gather(0, c.at[A], cbuf.at[y, A], right)
    from_right_b = gather(1, c.at[B], cbuf.at[y, B], left)

    loads[1].wait()
    fs[...] = split(f_v[...])
    loads[2].wait()
    pe[...] = fold(dot(fs[...], e_v[...], NT))
    loads[3].wait()
    loads[4].wait()
    a, u = gate_v[...].astype(f32), up_v[...].astype(f32)
    hidden = a * jax.nn.sigmoid(a) * u
    hidden = hidden.astype(bf16).astype(f32)
    hid[...] = hidden.astype(bf16)
    hid_t[...] = hidden.T.astype(bf16)

    from_left_b = gather(2, c.at[B], cbuf.at[y, B], right)
    from_right_a = gather(3, c.at[A], cbuf.at[y, A], left)

    def left_of_block(slot):
        block = fold(dot(fs[...], cbuf[slot], NT))
        return fold(dot(split(block), hid[pl.ds(pl.multiple_of(slot * rows, rows), rows), :]))

    loads[0].wait()
    pe[...] += left_of_block(y)

    from_left_a.wait_recv()
    from_opp_a = gather(4, cbuf.at[y_left, A], cbuf.at[y_left, A], right)
    from_right_b.wait_recv()
    from_opp_b = gather(5, cbuf.at[y_right, B], cbuf.at[y_right, B], left)
    from_left_b.wait_recv()
    pe[...] += left_of_block(y_left)
    from_right_a.wait_recv()
    pe[...] += left_of_block(y_right)
    for k in (5, 6, 7):
        loads[k].wait()
    from_opp_a.wait_recv()
    from_opp_b.wait_recv()
    p_all = left_of_block(y_opp) + pe[...]

    p1[...] = p_all.reshape(NZ, RANK // NZ, F)
    p1_copies = []
    for d in z_far:
        other = lax.rem(z + d, NZ)
        p1_copies.append(send(p1.at[other], p1_in.at[z], p1_s.at[d], p1_r.at[d], in_z(d)))
    p1_in[z] = p1[z]

    def weight_gradient(first):
        here = pl.ds(pl.multiple_of(first, qw), qw)
        block = cbuf[:, :, here].reshape(TOK, qw)
        value = dot(hid_t[...], block) + e_v[:, here].astype(f32)
        m_v[:, here] = value
        return value

    rest = pl.ds(1, NQ - 1)
    mc[0] = weight_gradient((1 - core) * hw).astype(bf16)
    mc_first = send(mc.at[0], mc_in.at[0], mc_s.at[0], mc_r.at[0], sibling)
    weight_gradient(core * hw)
    for q in range(1, NQ):
        mc[q] = weight_gradient((1 - core) * hw + q * qw).astype(bf16)
    mc_rest = send(mc.at[rest], mc_in.at[rest], mc_s.at[1], mc_r.at[1], sibling)

    def chip_sum(q):
        for k in range(NX):
            here = pl.ds(pl.multiple_of(core * hw + q * qw + k * pw, pw), pw)
            mx[k, q] = (m_v[:, here] + mc_in[q, :, k * pw : (k + 1) * pw].astype(f32)).astype(bf16)

    mc_first.wait_recv()
    chip_sum(0)
    mx_first, mx_rest = [], []
    for d in x_far:
        other = lax.rem(x + d, NX)
        mx_first.append(send(mx.at[other, 0], mx_in.at[x, 0], mx_s.at[0, d], mx_r.at[0, d], in_x(d)))

    def total_of(ref, count):
        total = ref[0].astype(f32)
        for k in range(1, count):
            total = total + ref[k].astype(f32)
        return total

    for copy in p1_copies:
        copy.wait_recv()
    p2_in[g] = total_of(p1_in, NZ)
    p2_copies = [send(p2_in.at[g], p2_in.at[g], p2_s.at[d], p2_r.at[d], in_group(d)) for d in g_far]

    for q in range(1, NQ):
        weight_gradient(core * hw + q * qw)
    mc_rest.wait_recv()
    for q in range(1, NQ):
        chip_sum(q)

    grad = dot(cbuf[...].reshape(TOK, D), wd_v[...], NT)
    a, u = gate_v[...].astype(f32), up_v[...].astype(f32)
    s = jax.nn.sigmoid(a)
    dg[...] = (grad * u * s * (1.0 + a * (1.0 - s))).astype(bf16)
    du[...] = (grad * (a * s)).astype(bf16)

    for copy in p2_copies:
        copy.wait_recv()
    t_v[z] = total_of(p2_in, G)
    p3_copies = [send(t_v.at[z], t_v.at[z], p3_s.at[d], p3_r.at[d], in_z(d)) for d in z_far]
    for d in x_far:
        other = lax.rem(x + d, NX)
        src, dst = mx.at[other, rest], mx_in.at[x, rest]
        mx_rest.append(send(src, dst, mx_s.at[1, d], mx_r.at[1, d], in_x(d)))
    mx_in[x] = mx[x]

    def part_tile(j):
        here = pl.ds(j * width, width)
        value = dot(dg[...], wg_v[here, :], NT) + dot(du[...], wu_v[here, :], NT)
        part[:, :, here] = value.astype(bf16).reshape(NY, rows, width)

    for j in range(D // width):
        part_tile(j)

    def give(k, src, to):
        return send(src, ig_in.at[k], ig_s.at[k], ig_r.at[k], to)

    ig0 = give(0, part.at[y_opp, A], right)
    ig3 = give(3, part.at[y_opp, B], left)
    ig1 = give(1, part.at[y_right, B], right)
    ig4 = give(4, part.at[y_left, A], left)
    for copy in p3_copies:
        copy.wait_recv()

    row_ids = lax.broadcasted_iota(jnp.int32, (RANK, 1), 0)
    tt[...] = t_v[...].reshape(RANK, F) * mean

    def column(k, carry):
        vector = tt[pl.ds(k, 1), :]
        tile = tt[...]
        squares = jnp.sum(vector * vector, axis=1, keepdims=True) + epsilon
        factors = jnp.sum(tile * vector, axis=1, keepdims=True) * (1.0 / squares)
        tt[...] = tile - jnp.where(row_ids > k, factors, 0.0) * vector
        tt[pl.ds(k, 1), :] = vector * lax.rsqrt(squares)
        return carry

    lax.fori_loop(0, RANK, column, 0)
    ts[...] = split(tt[...])

    for copy in mx_first + mx_rest:
        copy.wait_recv()
    m_sum = total_of(mx_in, NX)
    m_sum = jnp.concatenate([m_sum[q] for q in range(NQ)], axis=1)
    m_high = m_sum.astype(bf16)
    m_low = (m_sum - m_high.astype(f32)).astype(bf16)
    r_all = fold(dot(ts[...], m_high)) + dot(ts[:RANK], m_low)
    for k in range(NZ):
        q, h = k % 4, k // 4
        r2[k] = r_all[16 * q : 16 * q + 16, h * zw : (h + 1) * zw].astype(bf16)
    r2_copies = []
    for d in z_far:
        other = lax.rem(z + d, NZ)
        r2_copies.append(send(r2.at[other], r2_in.at[z], r2_s.at[d], r2_r.at[d], in_z(d)))
    r2_in[z] = r2[z]

    def all_left():
        for copy in sent:
            copy.wait_send()
        sent.clear()

    all_left()

    ig0.wait_recv()
    ig_sum[0] = (ig_in[0].astype(f32) + part[y_right, A].astype(f32)).astype(bf16)
    ig2 = give(2, ig_sum.at[0], right)
    ig3.wait_recv()
    ig_sum[1] = (ig_in[3].astype(f32) + part[y_left, B].astype(f32)).astype(bf16)
    ig5 = give(5, ig_sum.at[1], left)

    for copy in r2_copies:
        copy.wait_recv()
    rfull[core, x, z] = (total_of(r2_in, NZ) * mean).astype(bf16)
    own = rfull.at[core, x, z]
    r3_copies = {d: send(own, own, r3_s.at[d], r3_r.at[d], in_z(d)) for d in z_far}

    r4_copies = {}

    def along_x(k):
        piece = rfull.at[core, x, lax.rem(z + NZ - k, NZ)]
        for d in x_far:
            r4_copies[d, k] = send(piece, piece, r4_s.at[d, k], r4_r.at[d, k], in_x(d))

    along_x(0)
    for k in reversed(z_far):
        r3_copies[k].wait_recv()
        along_x(k)
    own = rfull.at[core, x]
    r5_copies = [send(own, own, r5_s.at[0], r5_r.at[0], sibling)]

    ig1.wait_recv()
    ig4.wait_recv()
    ig2.wait_recv()
    own_a = part[y, A].astype(f32) + ig_in[2].astype(f32) + ig_in[4].astype(f32)
    ig_v[A] = own_a.astype(bf16)
    ig5.wait_recv()
    own_b = part[y, B].astype(f32) + ig_in[1].astype(f32) + ig_in[5].astype(f32)
    ig_v[B] = own_b.astype(bf16)

    for d in reversed(x_far):
        for k in range(NZ):
            r4_copies[d, k].wait_recv()
        came = rfull.at[core, lax.rem(x + NX - d, NX)]
        r5_copies.append(send(came, came, r5_s.at[d], r5_r.at[d], sibling))
    for copy in sent:
        if not any(copy is last for last in r5_copies):
            copy.wait_send()
    for copy in r5_copies:
        copy.wait_recv()
    for copy in r5_copies:
        copy.wait_send()


def finish(ig_v, tt, rfull, m_v, ig, left_out, right_out, err, right_v, err_v, sems):
    RANK, F = tt.shape
    D = m_v.shape[1]
    hw = D // NC
    qw = hw // NQ
    pw = qw // NX
    zw = NQ * pw // (NZ // 4)
    copies = [
        pltpu.make_async_copy(ig_v, ig, sems.at[0]),
        pltpu.make_async_copy(tt, left_out, sems.at[1]),
    ]
    for copy in copies:
        copy.start()
    high = tt[...].astype(bf16).astype(f32)
    both = jnp.concatenate([high, tt[...] - high], axis=0).T.astype(bf16)
    for k in range(NC * NQ):
        h, at = divmod(k % NQ * pw, zw)
        blocks = []
        for chip in range(NX):
            rows = [rfull[k // NQ, chip, 4 * h + q, :, at : at + pw] for q in range(4)]
            blocks.append(jnp.concatenate(rows, axis=0))
        block = jnp.concatenate(blocks, axis=1)
        here = pl.ds(k * qw, qw)
        right_v[:, here] = block.astype(f32)
        update = dot(both, jnp.concatenate([block, block], axis=0))
        err_v[:, here] = (m_v[:, here] - update).astype(bf16)
        copies.append(pltpu.make_async_copy(err_v.at[:, here], err.at[:, here], sems.at[2 + 2 * k]))
        copies[-1].start()
        copies.append(pltpu.make_async_copy(right_v.at[:, here], right_out.at[:, here], sems.at[3 + 2 * k]))
        copies[-1].start()
    for copy in copies:
        copy.wait()


def shards(cotangent, gate_pre, up_pre, down_weight, gate_weight, up_weight, error_in, factor_in):
    G = NX * NC
    rows, D = cotangent.shape
    half = rows // 2
    TOK = NY * rows
    F = down_weight.shape[0]
    RANK = factor_in.shape[1]
    hw = D // NC
    qw = hw // NQ
    pw = qw // NX
    zw = NQ * pw // (NZ // 4)
    VM = pltpu.VMEM
    DMA = pltpu.SemaphoreType.DMA
    piece = RANK // NZ
    scratch = [
        VM((NY, rows, D), bf16), VM((F, D), bf16), VM((D, F), bf16), VM((D, F), bf16),
        VM((F, D), bf16), VM((RANK, D), f32), VM((2 * RANK, D), bf16),
        VM((TOK, F), bf16), VM((TOK, F), bf16), VM((TOK, F), bf16), VM((F, TOK), bf16),
        VM((RANK, F), f32), VM((TOK, F), bf16), VM((TOK, F), bf16),
        VM((NY, rows, D), bf16), VM((6, half, D), bf16), VM((2, half, D), bf16),
        VM((NZ, piece, F), f32), VM((NZ, piece, F), f32), VM((G, piece, F), f32), VM((NZ, piece, F), f32),
        VM((2 * RANK, F), bf16), VM((NQ, F, qw), bf16), VM((NQ, F, qw), bf16),
        VM((NX, NQ, F, pw), bf16), VM((NX, NQ, F, pw), bf16), VM((NZ, 16, zw), bf16), VM((NZ, 16, zw), bf16),
        DMA((8,)), DMA((6,)), DMA((6,)),
        DMA((NZ,)), DMA((NZ,)), DMA((G,)), DMA((G,)), DMA((NZ,)), DMA((NZ,)),
        DMA((2,)), DMA((2,)), DMA((2, NX)), DMA((2, NX)), DMA((NZ,)), DMA((NZ,)), DMA((NZ,)), DMA((NZ,)),
        DMA((NX, NZ)), DMA((NX, NZ)), DMA((NX,)), DMA((NX,)), DMA((6,)), DMA((6,)),
    ]
    in_vmem = pl.BlockSpec(memory_space=pltpu.VMEM)
    anywhere = pl.BlockSpec(memory_space=pl.ANY)
    held = pl.pallas_call(
        kernel,
        out_shape=(VM((rows, D), bf16), VM((RANK, F), f32), VM((NC, NX, NZ, 16, zw), bf16), VM((F, D), f32)),
        in_specs=[anywhere] * 8,
        out_specs=(in_vmem,) * 4,
        scratch_shapes=scratch,
        compiler_params=pltpu.CompilerParams(
            collective_id=0, has_side_effects=True, vmem_limit_bytes=VMEM_MIB * 1024 * 1024
        ),
        cost_estimate=pl.CostEstimate(flops=4 * 10**9, bytes_accessed=17 * 10**6, transcendentals=10**5),
    )(cotangent, gate_pre, up_pre, down_weight, gate_weight, up_weight, error_in[0], factor_in[0])
    shape = jax.ShapeDtypeStruct
    input_grad, left_t, right, error_out = pl.pallas_call(
        finish,
        out_shape=(shape((rows, D), bf16), shape((RANK, F), f32), shape((RANK, D), f32), shape((F, D), bf16)),
        in_specs=[in_vmem] * 4,
        out_specs=(anywhere,) * 4,
        scratch_shapes=[VM((RANK, D), f32), VM((F, D), bf16), DMA((2 + 2 * NC * NQ,))],
        compiler_params=pltpu.CompilerParams(vmem_limit_bytes=16 * 1024 * 1024),
        cost_estimate=pl.CostEstimate(flops=3 * 10**8, bytes_accessed=9 * 10**6, transcendentals=0),
    )(*held)
    return (input_grad, left_t.T, right[None], error_out[None])


def solution(mesh):
    in_specs = (
        P(("dp", "tensor"), None),
        P("dp", "tensor"),
        P("dp", "tensor"),
        P("tensor", None),
        P(None, "tensor"),
        P(None, "tensor"),
        P("dp", "tensor", None),
        P("tensor", None, None),
    )
    out_specs = (
        P(("dp", "tensor"), None),
        P("tensor", None),
        P("tensor", None, None),
        P("dp", "tensor", None),
    )
    return jax.shard_map(shards, mesh=mesh, in_specs=in_specs, out_specs=out_specs, check_vma=False)
```
